512 devices in a mesh: expert: 8 (over y), ffn: 32 (over x, z), dp: 2 (over core).
Axes of the slice: x: 4, y: 8, z: 8, core: 2. Of those that a mesh axis runs over, the one named last changes fastest.
Arguments:
- tokens: bfloat16 [2048, 2048], P(('expert', 'ffn'), 'dp'), may hold values from -6 to 6
- out_grad: bfloat16 [2048, 2048], P(('expert', 'ffn'), 'dp'), may hold values from -6 to 6
- expert_ids: int32 [2048, 2], P(('expert', 'ffn')), may hold values from 0 to 7, all different within a row; in each aligned block of 8 rows (0 to 7, 8 to 15, ...) at most 3 rows name the same one
- gate_probs: float32 [2048, 2], P(('expert', 'ffn')), may hold values from 0.1 to 1
- w_gate: bfloat16 [8, 2048, 8192], P('expert', 'dp', 'ffn'), may hold values from -0.125 to 0.125
- w_up: bfloat16 [8, 2048, 8192], P('expert', 'dp', 'ffn'), may hold values from -0.125 to 0.125
- w_down: bfloat16 [8, 8192, 2048], P('expert', 'ffn', 'dp'), may hold values from -0.0625 to 0.0625
Outputs:
- grad_tokens: bfloat16 [2048, 2048], P(('expert', 'ffn'), 'dp')
- grad_gate: bfloat16 [8, 2048, 8192], P('expert', 'dp', 'ffn')
- grad_up: bfloat16 [8, 2048, 8192], P('expert', 'dp', 'ffn')
- grad_down: bfloat16 [8, 8192, 2048], P('expert', 'ffn', 'dp')
- grad_probs: bfloat16 [2048, 2], P(('expert', 'ffn'))
The draws below stay inside these ranges and needn't reach their ends.
Inputs may be any that keep to these rules, and one draw needn't show every extreme that they name: `expert_ids`: within each aligned block of 8 tokens (the tokens of one index of expert and ffn), every expert is named by at most 3 pairs, a bound that some block reaches; the two ids of a token differ.
All inputs are finite; a program needn't handle non-finite values.
Results may differ from the reference program's by a relative error of at most 0.019.
Values may be sent and summed in bfloat16 or wider, within the bound.
No kernel may reach another device: no remote copies, remote signals or barrier semaphores. Data moves between devices by JAX's collectives and lax.ppermute only.
A program may use at most 64 MiB of HBM per device.

```python
import math
import jax
import jax.numpy as jnp
import numpy as np
from jax import lax

D = 2048
FF = 8192
TOK_DEV = 8
EXPERTS = 8
CAP = 3
TOKENS = 2048


def shard_levels(stream_key, extent, cuts, least, largest):
    loudness, own = 1.0, jax.random.fold_in(stream_key, 6)
    for position, parts in cuts:
        heights = jnp.exp(jax.random.uniform(jax.random.fold_in(own, position), (parts,), jnp.float32, least / len(cuts), largest / len(cuts)))
        loudness = loudness * jnp.repeat(heights, extent[position] // parts).reshape([-1 if axis == position else 1 for axis in range(len(extent))])
    return loudness


def shared_out(rng, own, number, rows, count, top, most, lean):
    ranking = jax.random.permutation(rng, count)
    packed, usual = portions_of(count, rows * top, most, lean, True), portions_of(count, rows * top, most, lean, False)
    places = jnp.arange(count)

    def named(tallies, offset_by):
        used = int((tallies > 0).sum())
        fixed = max(1, used // 4)
        passed = fixed + (places - fixed + offset_by * (used - fixed)) % max(1, count - fixed)
        return jnp.zeros((count,), jnp.int32).at[ranking[jnp.where(places < fixed, places, passed)]].set(jnp.asarray(tallies, jnp.int32))

    tallies = jnp.where(number % 4 == 0, named(packed, number // 4), named(usual, number - number // 4 - 1))
    mixed = jax.random.permutation(jax.random.fold_in(own, 3), count)
    source_of, taker = mixed[0:count // 2 * 2:2], mixed[1:count // 2 * 2:2]
    room = jnp.minimum(tallies[source_of] - 1, most - tallies[taker]) // 2
    room = jnp.where((source_of == ranking[0]) | (taker == ranking[0]) | (tallies[taker] == 0), 0, jnp.maximum(room, 0))
    passed = jax.random.randint(jax.random.fold_in(own, 4), (count // 2,), 0, 1 << 20) % (room + 1)
    tallies = tallies.at[source_of].add(-passed).at[taker].add(passed)
    members = jnp.searchsorted(jnp.cumsum(tallies), jnp.arange(rows * top), side="right").astype(jnp.int32)
    listing = members.reshape(top, rows).T
    listing = listing[jax.random.permutation(jax.random.fold_in(own, 1), rows)]
    offset_by = jax.random.randint(jax.random.fold_in(own, 2), (rows, 1), 0, top)
    return jnp.take_along_axis(listing, (jnp.arange(top)[None, :] + offset_by) % top, axis=1)


def portions_of(amount, total, limit, skew, full):
    weights = [(1 << 20) // math.isqrt(grade ** skew) + 1 for grade in range(1, amount + 1)]
    largest = limit if full else min(limit, max(-(-total // amount), total * weights[0] // sum(weights)))
    least = 1 if total - largest >= amount - 1 else 0
    given, spare = [largest] + [least] * (amount - 1), total - largest - least * (amount - 1)
    while spare > 0:
        free = [i for i in range(1, amount) if given[i] < largest] or [i for i in range(1, amount) if given[i] < limit]
        pool, left = sum([weights[i] for i in free]), spare
        for i in free:
            extra = min(limit - given[i], max(1, left * weights[i] // pool), spare)
            given[i] = given[i] + extra
            spare = spare - extra
    return np.array(given)


def gaussian(key, extent, deviation, limit, shards=(), kind=jnp.bfloat16):
    loudness = shard_levels(key, extent, shards, -0.22, 0.18) if shards else 1.0
    array = jax.random.normal(key, extent, jnp.float32) * deviation * loudness
    return jnp.minimum(jnp.maximum(array, -limit), limit).astype(kind)


def setup_inputs(seed: int = 0) -> dict:
    keys = jax.random.split(jax.random.key(seed), 8)
    tokens = gaussian(keys[0], (TOKENS, D), 1.0, 6.0, ((0, 256), (1, 2)))
    out_grad = gaussian(keys[1], (TOKENS, D), 1.0, 6.0, ((0, 256), (1, 2)))
    expert_ids_keys = jax.random.split(jax.random.fold_in(keys[2], 1), TOKENS // TOK_DEV)
    expert_ids_turns = jax.random.permutation(jax.random.fold_in(keys[2], 3), TOKENS // TOK_DEV)
    expert_ids = jax.vmap(lambda own, number: shared_out(jax.random.fold_in(keys[2], 2), own, number, TOK_DEV, EXPERTS, 2, CAP, 2))(expert_ids_keys, expert_ids_turns).reshape((TOKENS, 2))
    gate_probs = jnp.clip(0.1 + 0.9 * jax.random.uniform(keys[3], (TOKENS, 2), jnp.float32) ** shard_levels(keys[3], (TOKENS, 2), ((0, 256),), -0.2, 0.2), 0.1, 1.0)
    w_gate = gaussian(keys[4], (EXPERTS, D, FF), D ** -0.5, 0.125, ((0, 8), (1, 2), (2, 32)))
    w_up = gaussian(keys[5], (EXPERTS, D, FF), D ** -0.5, 0.125, ((0, 8), (1, 2), (2, 32)))
    w_down = gaussian(keys[6], (EXPERTS, FF, D), FF ** -0.5, 0.0625, ((0, 8), (1, 32), (2, 2)))
    return dict(tokens=tokens, out_grad=out_grad, expert_ids=expert_ids, gate_probs=gate_probs, w_gate=w_gate, w_up=w_up, w_down=w_down)


def reference(tokens, out_grad, expert_ids, gate_probs, w_gate, w_up, w_down):
    groups = TOKENS // TOK_DEV
    pairs = TOK_DEV * 2
    ids = expert_ids.reshape(groups, pairs).astype(jnp.int32)
    names = jnp.arange(EXPERTS, dtype=jnp.int32)
    onehot = (ids[:, :, None] == names[None, None, :]).astype(jnp.int32)
    slots = jnp.sum((jnp.cumsum(onehot, axis=1) - onehot) * onehot, axis=2).astype(jnp.int32)
    group_index = jnp.broadcast_to(jnp.arange(groups, dtype=jnp.int32)[:, None], (groups, pairs))
    pair_index = (group_index * pairs + jnp.arange(pairs, dtype=jnp.int32)[None, :]).astype(jnp.int32)
    table = jnp.full((EXPERTS, groups, CAP), 2 * TOKENS, jnp.int32)
    table = table.at[ids, group_index, slots].set(pair_index)
    probs = jnp.concatenate([gate_probs.astype(jnp.bfloat16).reshape(-1), jnp.zeros((1,), jnp.bfloat16)])
    padded_x = jnp.concatenate([tokens, jnp.zeros((1, D), jnp.bfloat16)])
    padded_dy = jnp.concatenate([out_grad, jnp.zeros((1, D), jnp.bfloat16)])

    def expert_step(carry, inputs):
        grad_acc, score_acc = carry
        gate_w, up_w, down_w, slot_rows = inputs
        rows = slot_rows.reshape(-1).astype(jnp.int32)
        owner = (rows // 2).astype(jnp.int32)
        inputs_x = padded_x[owner]
        inputs_dy = padded_dy[owner]
        weight = probs[rows].astype(jnp.float32)
        gate_pre = jnp.dot(inputs_x, gate_w, preferred_element_type=jnp.float32)
        up_pre = jnp.dot(inputs_x, up_w, preferred_element_type=jnp.float32)
        backward = jnp.dot(inputs_dy, down_w.T, preferred_element_type=jnp.float32)
        sigmoid_gate = jax.nn.sigmoid(gate_pre)
        silu_gate = gate_pre * sigmoid_gate
        hidden = (silu_gate * up_pre).astype(jnp.bfloat16)
        score = jnp.sum(backward * hidden.astype(jnp.float32), axis=1)
        scaled = (weight[:, None] * inputs_dy.astype(jnp.float32)).astype(jnp.bfloat16)
        d_hidden = weight[:, None] * backward
        grad_gate_pre = (d_hidden * up_pre * sigmoid_gate * (1.0 + gate_pre * (1.0 - sigmoid_gate))).astype(jnp.bfloat16)
        grad_up_pre = (d_hidden * silu_gate).astype(jnp.bfloat16)
        gate_grad = jnp.dot(inputs_x.T, grad_gate_pre, preferred_element_type=jnp.float32).astype(jnp.bfloat16)
        up_grad = jnp.dot(inputs_x.T, grad_up_pre, preferred_element_type=jnp.float32).astype(jnp.bfloat16)
        down_grad = jnp.dot(hidden.T, scaled, preferred_element_type=jnp.float32).astype(jnp.bfloat16)
        pair_grad = (jnp.dot(grad_gate_pre, gate_w.T, preferred_element_type=jnp.float32)
                     + jnp.dot(grad_up_pre, up_w.T, preferred_element_type=jnp.float32)).astype(jnp.bfloat16)
        grad_acc = grad_acc.at[owner].add(pair_grad.astype(jnp.float32))
        score_acc = score_acc.at[rows].add(score)
        return (grad_acc, score_acc), (gate_grad, up_grad, down_grad)

    start = (jnp.zeros((TOKENS + 1, D), jnp.float32), jnp.zeros((2 * TOKENS + 1,), jnp.float32))
    (grad_acc, score_acc), (grad_gate, grad_up, grad_down) = lax.scan(
        expert_step, start, (w_gate, w_up, w_down, table))
    grad_tokens = grad_acc[:TOKENS].astype(jnp.bfloat16)
    grad_probs = score_acc[:2 * TOKENS].reshape(TOKENS, 2).astype(jnp.bfloat16)
    return (grad_tokens, grad_gate, grad_up, grad_down, grad_probs)
```

```python
import jax
import jax.numpy as jnp
from jax import lax
from jax.sharding import Mesh
from jax.sharding import PartitionSpec as P

CAP = 3
LANES = 128


def contract(left, right, left_dim, right_dim):
    return lax.dot_general(
        left, right, (((left_dim,), (right_dim,)), ((), ())), preferred_element_type=jnp.float32
    )


def exchange(block, axes):
    return lax.all_to_all(block, axes, split_axis=0, concat_axis=0, tiled=True)


def per_device(tokens, out_grad, expert_ids, gate_probs, w_gate, w_up, w_down):
    experts = lax.axis_size("expert")
    nx = lax.axis_size("x")
    nz = lax.axis_size("z")
    tok_rows, width = tokens.shape
    chunks = width // LANES
    slots = experts * CAP

    flat_ids = expert_ids.reshape(-1)
    onehot = (flat_ids[:, None] == jnp.arange(experts, dtype=jnp.int32)[None, :]).astype(jnp.int32)
    earlier = jnp.tril(jnp.ones((2 * tok_rows, 2 * tok_rows), jnp.int32), -1)
    same = (flat_ids[:, None] == flat_ids[None, :]).astype(jnp.int32)
    ranks = jnp.sum(same * earlier, axis=1)
    position = (flat_ids * CAP + ranks).reshape(tok_rows, 2)
    slot_names = jnp.arange(slots, dtype=jnp.int32)
    place0 = slot_names[:, None] == position[None, :, 0]
    place1 = slot_names[:, None] == position[None, :, 1]
    placing = (place0 | place1).astype(jnp.bfloat16)
    probs = gate_probs.astype(jnp.bfloat16).astype(jnp.float32)
    slot_prob = jnp.sum(
        jnp.where(place0, probs[None, :, 0], 0.0) + jnp.where(place1, probs[None, :, 1], 0.0),
        axis=1,
        keepdims=True,
    )
    send_x = contract(placing, tokens, 1, 0).astype(jnp.bfloat16)
    send_dy = (contract(placing, out_grad, 1, 0) * slot_prob).astype(jnp.bfloat16)
    send = jnp.concatenate([send_x, send_dy], axis=1)
    send = send.reshape(experts, 1, CAP * 2 * chunks, LANES)
    send = jnp.broadcast_to(send, (experts, nz, CAP * 2 * chunks, LANES))
    send = send.reshape(experts * nz, CAP * 2 * chunks, LANES)

    recv = exchange(send, ("expert", "z"))
    part_rows = experts * nz * CAP
    block = recv.reshape(part_rows, 2 * width)
    block = jnp.broadcast_to(block[None], (nx, part_rows, 2 * width))
    rows = exchange(block, "x").reshape(nx * part_rows, 2 * width)
    rows_x = rows[:, :width]
    rows_dy = rows[:, width:]

    gate_w = w_gate[0]
    up_w = w_up[0]
    down_w = w_down[0]
    partial = jnp.concatenate(
        [
            contract(rows_x, gate_w, 1, 0),
            contract(rows_x, up_w, 1, 0),
            contract(rows_dy, down_w, 1, 1),
        ],
        axis=1,
    ).astype(jnp.bfloat16)
    other = lax.ppermute(partial, "dp", [(0, 1), (1, 0)])
    total = partial.astype(jnp.float32) + other.astype(jnp.float32)
    hid = gate_w.shape[1]
    gate_pre, up_pre, d_hidden = total[:, :hid], total[:, hid : 2 * hid], total[:, 2 * hid :]

    sigmoid_gate = jax.nn.sigmoid(gate_pre)
    silu_gate = gate_pre * sigmoid_gate
    hidden = (silu_gate * up_pre).astype(jnp.bfloat16)
    score = jnp.sum(d_hidden * hidden.astype(jnp.float32), axis=1)
    grad_gate_pre = (
        d_hidden * up_pre * sigmoid_gate * (1.0 + gate_pre * (1.0 - sigmoid_gate))
    ).astype(jnp.bfloat16)
    grad_up_pre = (d_hidden * silu_gate).astype(jnp.bfloat16)

    input_part = (
        contract(grad_gate_pre, gate_w, 1, 1) + contract(grad_up_pre, up_w, 1, 1)
    ).astype(jnp.bfloat16)
    score_rows = score.astype(jnp.bfloat16).reshape(nx, 1, part_rows)
    score_rows = jnp.pad(score_rows, ((0, 0), (0, 7), (0, width - part_rows)))
    back = jnp.concatenate([input_part.reshape(nx, part_rows, width), score_rows], axis=1)
    back = exchange(back.reshape(nx * (part_rows + 8), width), "x")
    back = jnp.sum(back.reshape(nx, part_rows + 8, width).astype(jnp.float32), axis=0)
    back = back.astype(jnp.bfloat16)

    grad_gate = contract(rows_x, grad_gate_pre, 0, 0).astype(jnp.bfloat16)[None]
    grad_up = contract(rows_x, grad_up_pre, 0, 0).astype(jnp.bfloat16)[None]
    grad_down = contract(hidden, rows_dy, 0, 0).astype(jnp.bfloat16)[None]

    data = back[:part_rows].reshape(experts * nz, CAP * chunks, LANES)
    marks = jnp.pad(
        back[part_rows, :part_rows].reshape(experts * nz, 1, CAP),
        ((0, 0), (0, 7), (0, LANES - CAP)),
    )
    home = exchange(jnp.concatenate([data, marks], axis=1), ("expert", "z"))
    home = jnp.sum(
        home.reshape(experts, nz, CAP * chunks + 8, LANES).astype(jnp.float32), axis=1
    )
    pair_rows = home[:, : CAP * chunks].astype(jnp.bfloat16).reshape(slots, width)
    pair_score = home[:, CAP * chunks, :CAP].reshape(slots, 1)
    grad_tokens = contract(placing, pair_rows, 0, 0).astype(jnp.bfloat16)
    score0 = jnp.sum(jnp.where(place0, pair_score, 0.0), axis=0)
    score1 = jnp.sum(jnp.where(place1, pair_score, 0.0), axis=0)
    grad_probs = (jnp.stack([score0, score1], axis=1) / probs).astype(jnp.bfloat16)
    return (grad_tokens, grad_gate, grad_up, grad_down, grad_probs)


def solution(mesh):
    names = dict(zip(mesh.axis_names, mesh.devices.shape))
    nz = 8
    nx = names["ffn"] // nz
    grid = Mesh(
        mesh.devices.reshape(names["expert"], nx, nz, names["dp"]), ("expert", "x", "z", "dp")
    )
    toks = P(("expert", "x", "z"), "dp")
    pairs = P(("expert", "x", "z"), None)
    wide = P("expert", "dp", ("x", "z"))
    tall = P("expert", ("x", "z"), "dp")
    return jax.shard_map(
        per_device,
        mesh=grid,
        in_specs=(toks, toks, pairs, pairs, wide, wide, tall),
        out_specs=(toks, wide, wide, tall, pairs),
        check_vma=False,
    )
```

```python
import jax
import jax.numpy as jnp
from jax import lax
from jax.sharding import Mesh
from jax.sharding import PartitionSpec as P

CAP = 3
LANES = 128


def contract(left, right, left_dim, right_dim):
    return lax.dot_general(
        left, right, (((left_dim,), (right_dim,)), ((), ())), preferred_element_type=jnp.float32
    )


def exchange(block, axes):
    return lax.all_to_all(block, axes, split_axis=0, concat_axis=0, tiled=True)


def per_device(tokens, out_grad, expert_ids, gate_probs, w_gate, w_up, w_down):
    experts = lax.axis_size("expert")
    nx = lax.axis_size("x")
    nz = lax.axis_size("z")
    tok_rows, width = tokens.shape
    chunks = width // LANES
    slots = experts * CAP

    flat_ids = expert_ids.reshape(-1)
    onehot = (flat_ids[:, None] == jnp.arange(experts, dtype=jnp.int32)[None, :]).astype(jnp.int32)
    earlier = jnp.tril(jnp.ones((2 * tok_rows, 2 * tok_rows), jnp.int32), -1)
    same = (flat_ids[:, None] == flat_ids[None, :]).astype(jnp.int32)
    ranks = jnp.sum(same * earlier, axis=1)
    position = (flat_ids * CAP + ranks).reshape(tok_rows, 2)
    slot_names = jnp.arange(slots, dtype=jnp.int32)
    place0 = slot_names[:, None] == position[None, :, 0]
    place1 = slot_names[:, None] == position[None, :, 1]
    placing = (place0 | place1).astype(jnp.bfloat16)
    probs = gate_probs.astype(jnp.bfloat16).astype(jnp.float32)
    slot_prob = jnp.sum(
        jnp.where(place0, probs[None, :, 0], 0.0) + jnp.where(place1, probs[None, :, 1], 0.0),
        axis=1,
        keepdims=True,
    )
    send_x = contract(placing, tokens, 1, 0).astype(jnp.bfloat16)
    send_dy = (contract(placing, out_grad, 1, 0) * slot_prob).astype(jnp.bfloat16)
    send = jnp.concatenate([send_x, send_dy], axis=1)
    send = send.reshape(experts, 1, CAP * 2 * chunks, LANES)
    send = jnp.broadcast_to(send, (experts, nz, CAP * 2 * chunks, LANES))
    send = send.reshape(experts * nz, CAP * 2 * chunks, LANES)

    recv = exchange(send, ("expert", "z"))
    part_rows = experts * nz * CAP
    block = recv.reshape(part_rows, 2 * width)
    rows_dy = lax.all_gather(block[:, width:], "x", axis=0, tiled=True)
    block = jnp.broadcast_to(block[None, :, :width], (nx, part_rows, width))
    rows_x = exchange(block, "x").reshape(nx * part_rows, width)

    gate_w = w_gate[0]
    up_w = w_up[0]
    down_w = w_down[0]
    hid = gate_w.shape[1]

    def both(partial):
        partial = partial.astype(jnp.bfloat16)
        other = lax.ppermute(partial, "dp", [(0, 1), (1, 0)])
        return partial.astype(jnp.float32) + other.astype(jnp.float32)

    pre = both(
        jnp.concatenate([contract(rows_x, gate_w, 1, 0), contract(rows_x, up_w, 1, 0)], axis=1)
    )
    gate_pre, up_pre = pre[:, :hid], pre[:, hid:]
    d_hidden = both(contract(rows_dy, down_w, 1, 1))

    sigmoid_gate = jax.nn.sigmoid(gate_pre)
    silu_gate = gate_pre * sigmoid_gate
    hidden = (silu_gate * up_pre).astype(jnp.bfloat16)
    score = jnp.sum(d_hidden * hidden.astype(jnp.float32), axis=1)
    grad_gate_pre = (
        d_hidden * up_pre * sigmoid_gate * (1.0 + gate_pre * (1.0 - sigmoid_gate))
    ).astype(jnp.bfloat16)
    grad_up_pre = (d_hidden * silu_gate).astype(jnp.bfloat16)

    input_part = (
        contract(grad_gate_pre, gate_w, 1, 1) + contract(grad_up_pre, up_w, 1, 1)
    ).astype(jnp.bfloat16)
    score_rows = score.astype(jnp.bfloat16).reshape(nx, 1, part_rows)
    score_rows = jnp.pad(score_rows, ((0, 0), (0, 7), (0, width - part_rows)))
    back = jnp.concatenate([input_part.reshape(nx, part_rows, width), score_rows], axis=1)
    back = exchange(back.reshape(nx * (part_rows + 8), width), "x")
    back = jnp.sum(back.reshape(nx, part_rows + 8, width).astype(jnp.float32), axis=0)
    back = back.astype(jnp.bfloat16)

    grad_gate = contract(rows_x, grad_gate_pre, 0, 0).astype(jnp.bfloat16)[None]
    grad_up = contract(rows_x, grad_up_pre, 0, 0).astype(jnp.bfloat16)[None]
    grad_down = contract(hidden, rows_dy, 0, 0).astype(jnp.bfloat16)[None]

    data = back[:part_rows].reshape(experts * nz, CAP * chunks, LANES)
    marks = jnp.pad(
        back[part_rows, :part_rows].reshape(experts * nz, 1, CAP),
        ((0, 0), (0, 1), (0, LANES - CAP)),
    )
    home = jnp.concatenate([data, marks], axis=1)
    home = exchange(
        home.reshape(experts * nz, CAP * chunks // 2 + 1, 2, LANES), ("expert", "z")
    )
    home = jnp.sum(
        home.reshape(experts, nz, CAP * chunks + 2, LANES).astype(jnp.float32), axis=1
    )
    pair_rows = home[:, : CAP * chunks].astype(jnp.bfloat16).reshape(slots, width)
    pair_score = home[:, CAP * chunks, :CAP].reshape(slots, 1)
    grad_tokens = contract(placing, pair_rows, 0, 0).astype(jnp.bfloat16)
    score0 = jnp.sum(jnp.where(place0, pair_score, 0.0), axis=0)
    score1 = jnp.sum(jnp.where(place1, pair_score, 0.0), axis=0)
    grad_probs = (jnp.stack([score0, score1], axis=1) / probs).astype(jnp.bfloat16)
    return (grad_tokens, grad_gate, grad_up, grad_down, grad_probs)


def solution(mesh):
    names = dict(zip(mesh.axis_names, mesh.devices.shape))
    nz = 8
    nx = names["ffn"] // nz
    grid = Mesh(
        mesh.devices.reshape(names["expert"], nx, nz, names["dp"]), ("expert", "x", "z", "dp")
    )
    toks = P(("expert", "x", "z"), "dp")
    pairs = P(("expert", "x", "z"), None)
    wide = P("expert", "dp", ("x", "z"))
    tall = P("expert", ("x", "z"), "dp")
    return jax.shard_map(
        per_device,
        mesh=grid,
        in_specs=(toks, toks, pairs, pairs, wide, wide, tall),
        out_specs=(toks, wide, wide, tall, pairs),
        check_vma=False,
    )
```

```python
import jax
import jax.numpy as jnp
from jax import lax
from jax.sharding import Mesh
from jax.sharding import PartitionSpec as P

CAP = 3
LANES = 128


def contract(left, right, left_dim, right_dim):
    return lax.dot_general(
        left, right, (((left_dim,), (right_dim,)), ((), ())), preferred_element_type=jnp.float32
    )


def exchange(block, axes):
    return lax.all_to_all(block, axes, split_axis=0, concat_axis=0, tiled=True)


def per_device(tokens, out_grad, expert_ids, gate_probs, w_gate, w_up, w_down):
    experts = lax.axis_size("expert")
    nx = lax.axis_size("x")
    nz = lax.axis_size("z")
    tok_rows, width = tokens.shape
    chunks = width // LANES
    slots = experts * CAP

    flat_ids = expert_ids.reshape(-1)
    onehot = (flat_ids[:, None] == jnp.arange(experts, dtype=jnp.int32)[None, :]).astype(jnp.int32)
    earlier = jnp.tril(jnp.ones((2 * tok_rows, 2 * tok_rows), jnp.int32), -1)
    same = (flat_ids[:, None] == flat_ids[None, :]).astype(jnp.int32)
    ranks = jnp.sum(same * earlier, axis=1)
    position = (flat_ids * CAP + ranks).reshape(tok_rows, 2)
    slot_names = jnp.arange(slots, dtype=jnp.int32)
    place0 = slot_names[:, None] == position[None, :, 0]
    place1 = slot_names[:, None] == position[None, :, 1]
    placing = (place0 | place1).astype(jnp.bfloat16)
    probs = gate_probs.astype(jnp.bfloat16).astype(jnp.float32)
    slot_prob = jnp.sum(
        jnp.where(place0, probs[None, :, 0], 0.0) + jnp.where(place1, probs[None, :, 1], 0.0),
        axis=1,
        keepdims=True,
    )
    send_x = contract(placing, tokens, 1, 0).astype(jnp.bfloat16)
    send_dy = (contract(placing, out_grad, 1, 0) * slot_prob).astype(jnp.bfloat16)
    send = jnp.concatenate([send_x, send_dy], axis=1)
    send = send.reshape(experts, 1, CAP * 2 * chunks, LANES)
    send = jnp.broadcast_to(send, (experts, nz, CAP * 2 * chunks, LANES))
    send = send.reshape(experts * nz, CAP * 2 * chunks, LANES)

    part_rows = experts * nz * CAP
    gate_w = w_gate[0]
    up_w = w_up[0]
    down_w = w_down[0]
    hid = gate_w.shape[1]

    def meet(block, mask):
        return lax.ppermute(block, "x", [(i, i ^ mask) for i in range(nx)])

    def swap(block):
        return lax.ppermute(block, "dp", [(0, 1), (1, 0)])

    def stacked(gate, up, down):
        return jnp.concatenate([gate, up] + jnp.split(down, width // hid, axis=1), axis=0)

    def unstacked(stack):
        gate, up, down = jnp.split(stack, 3, axis=0)
        return gate, up, jnp.concatenate(jnp.split(down, width // hid, axis=0), axis=1)

    gate_n, up_n, down_n = unstacked(meet(stacked(gate_w, up_w, down_w), 1))
    gate_w = jnp.concatenate([gate_w, gate_n], axis=1)
    up_w = jnp.concatenate([up_w, up_n], axis=1)
    down_w = jnp.concatenate([down_w, down_n], axis=0)

    def project(rows):
        return jnp.concatenate(
            [
                contract(rows[:, :width], gate_w, 1, 0),
                contract(rows[:, :width], up_w, 1, 0),
                contract(rows[:, width:], down_w, 1, 1),
            ],
            axis=1,
        ).astype(jnp.bfloat16)

    def pullback(partial, other):
        total = partial.astype(jnp.float32) + other.astype(jnp.float32)
        gate_pre, up_pre, d_hidden = jnp.split(total, 3, axis=1)
        sigmoid_gate = jax.nn.sigmoid(gate_pre)
        silu_gate = gate_pre * sigmoid_gate
        hidden = (silu_gate * up_pre).astype(jnp.bfloat16)
        score = jnp.sum(d_hidden * hidden.astype(jnp.float32), axis=1)
        grad_gate_pre = (
            d_hidden * up_pre * sigmoid_gate * (1.0 + gate_pre * (1.0 - sigmoid_gate))
        ).astype(jnp.bfloat16)
        grad_up_pre = (d_hidden * silu_gate).astype(jnp.bfloat16)
        input_part = (
            contract(grad_gate_pre, gate_w, 1, 1) + contract(grad_up_pre, up_w, 1, 1)
        ).astype(jnp.bfloat16)
        return hidden, grad_gate_pre, grad_up_pre, input_part, score.astype(jnp.bfloat16)

    def packed(input_part, score):
        score_row = jnp.pad(score.reshape(1, part_rows), ((0, 7), (0, width - part_rows)))
        return jnp.concatenate([input_part, score_row], axis=0)

    own = exchange(send, ("expert", "z")).reshape(part_rows, 2 * width)
    guest = meet(own, 3)
    own, guest = lax.optimization_barrier((own, guest))
    rows = jnp.concatenate([guest, own], axis=0)
    partial = project(rows)
    hidden, grad_gate_pre, grad_up_pre, input_part, score = pullback(partial, swap(partial))
    back = meet(packed(input_part[:part_rows], score[:part_rows]), 3)
    back = (
        packed(input_part[part_rows:], score[part_rows:]).astype(jnp.float32)
        + back.astype(jnp.float32)
    ).astype(jnp.bfloat16)
    rows_x, rows_dy = rows[:, :width], rows[:, width:]

    def weight_grads(part):
        return (
            contract(rows_x, grad_gate_pre[:, part], 0, 0),
            contract(rows_x, grad_up_pre[:, part], 0, 0),
            contract(hidden[:, part], rows_dy, 0, 0),
        )

    theirs = [g.astype(jnp.bfloat16) for g in weight_grads(slice(hid, None))]
    theirs = unstacked(meet(stacked(*theirs), 1))
    grad_gate, grad_up, grad_down = (
        (mine + other.astype(jnp.float32)).astype(jnp.bfloat16)[None]
        for mine, other in zip(weight_grads(slice(0, hid)), theirs)
    )

    data = back[:part_rows].reshape(experts * nz, CAP * chunks, LANES)
    marks = jnp.pad(
        back[part_rows, :part_rows].reshape(experts * nz, 1, CAP),
        ((0, 0), (0, 1), (0, LANES - CAP)),
    )
    home = jnp.concatenate([data, marks], axis=1)
    home = exchange(
        home.reshape(experts * nz, CAP * chunks // 2 + 1, 2, LANES), ("expert", "z")
    )
    home = jnp.sum(
        home.reshape(experts, nz, CAP * chunks + 2, LANES).astype(jnp.float32), axis=1
    )
    pair_rows = home[:, : CAP * chunks].astype(jnp.bfloat16).reshape(slots, width)
    pair_score = home[:, CAP * chunks, :CAP].reshape(slots, 1)
    grad_tokens = contract(placing, pair_rows, 0, 0).astype(jnp.bfloat16)
    score0 = jnp.sum(jnp.where(place0, pair_score, 0.0), axis=0)
    score1 = jnp.sum(jnp.where(place1, pair_score, 0.0), axis=0)
    grad_probs = (jnp.stack([score0, score1], axis=1) / probs).astype(jnp.bfloat16)
    return (grad_tokens, grad_gate, grad_up, grad_down, grad_probs)


def solution(mesh):
    names = dict(zip(mesh.axis_names, mesh.devices.shape))
    nz = 8
    nx = names["ffn"] // nz
    grid = Mesh(
        mesh.devices.reshape(names["expert"], nx, nz, names["dp"]), ("expert", "x", "z", "dp")
    )
    toks = P(("expert", "x", "z"), "dp")
    pairs = P(("expert", "x", "z"), None)
    wide = P("expert", "dp", ("x", "z"))
    tall = P("expert", ("x", "z"), "dp")
    return jax.shard_map(
        per_device,
        mesh=grid,
        in_specs=(toks, toks, pairs, pairs, wide, wide, tall),
        out_specs=(toks, wide, wide, tall, pairs),
        check_vma=False,
    )
```

```python
import jax
import jax.numpy as jnp
from jax import lax
from jax.experimental import pallas as pl
from jax.experimental.pallas import tpu as pltpu
from jax.sharding import Mesh
from jax.sharding import PartitionSpec as P

CAP = 3
LANES = 128


def contract(left, right, left_dim, right_dim):
    return lax.dot_general(
        left, right, (((left_dim,), (right_dim,)), ((), ())), preferred_element_type=jnp.float32
    )


def exchange(block, axes):
    return lax.all_to_all(block, axes, split_axis=0, concat_axis=0, tiled=True)


def dispatch_kernel(ids_ref, probs_ref, tokens_ref, out_grad_ref, send_ref, position_ref, stage_ref):
    experts, nz = send_ref.shape[0], send_ref.shape[1]
    toks, width = tokens_ref.shape
    chunks = width // LANES
    ids = [ids_ref[k : k + 1, :] for k in range(2)]
    probs = [probs_ref[k : k + 1, :].astype(jnp.bfloat16).astype(jnp.float32) for k in range(2)]
    a = lax.broadcasted_iota(jnp.int32, (toks, toks), 0)
    b = lax.broadcasted_iota(jnp.int32, (toks, toks), 1)
    columns = [
        jnp.sum(jnp.where(a == b, jnp.broadcast_to(i, (toks, toks)), 0), axis=1, keepdims=True)
        for i in ids
    ]
    places = []
    for k in range(2):
        rank = jnp.zeros((1, toks), jnp.int32)
        for other in range(2):
            earlier = (a < b) if other >= k else (a <= b)
            match = (columns[other] == ids[k]) & earlier
            rank = rank + jnp.sum(match.astype(jnp.int32), axis=0, keepdims=True)
        position_ref[k : k + 1, :] = ids[k] * CAP + rank
        places.append((ids[k], rank))
    names = lax.broadcasted_iota(jnp.int32, (experts, toks), 0)
    x = tokens_ref[...].astype(jnp.float32)
    dy = out_grad_ref[...].astype(jnp.float32)
    for slot in range(CAP):
        masks = [(names == i) & (rank == slot) for i, rank in places]
        hit = (masks[0] | masks[1]).astype(jnp.float32)
        weight = jnp.sum(
            jnp.where(masks[0], probs[0], 0.0) + jnp.where(masks[1], probs[1], 0.0),
            axis=1,
            keepdims=True,
        )
        rows_x = jnp.zeros((experts, width), jnp.float32)
        rows_dy = jnp.zeros((experts, width), jnp.float32)
        for t in range(toks):
            rows_x = rows_x + hit[:, t : t + 1] * x[t : t + 1, :]
            rows_dy = rows_dy + hit[:, t : t + 1] * dy[t : t + 1, :]
        rows_dy = rows_dy * weight
        for c in range(chunks):
            lanes = slice(c * LANES, (c + 1) * LANES)
            stage_ref[:, slot * 2 * chunks + c, :] = rows_x[:, lanes]
            stage_ref[:, slot * 2 * chunks + chunks + c, :] = rows_dy[:, lanes]
    for e in range(experts):
        block = stage_ref[e].astype(jnp.bfloat16)
        for z in range(nz):
            send_ref[e, z] = block


def per_device(tokens, out_grad, expert_ids, gate_probs, w_gate, w_up, w_down):
    experts = lax.axis_size("expert")
    nx = lax.axis_size("x")
    nz = lax.axis_size("z")
    tok_rows, width = tokens.shape
    chunks = width // LANES
    slots = experts * CAP

    probs = gate_probs.astype(jnp.bfloat16).astype(jnp.float32)
    rows_out = CAP * 2 * chunks
    send, position = pl.pallas_call(
        dispatch_kernel,
        out_shape=(
            jax.ShapeDtypeStruct((experts, nz, rows_out, LANES), jnp.bfloat16),
            jax.ShapeDtypeStruct((2, tok_rows), jnp.int32),
        ),
        in_specs=[pl.BlockSpec(memory_space=pltpu.VMEM)] * 4,
        out_specs=(
            pl.BlockSpec(memory_space=pltpu.VMEM),
            pl.BlockSpec(memory_space=pltpu.VMEM),
        ),
        scratch_shapes=[pltpu.VMEM((experts, rows_out, LANES), jnp.float32)],
    )(expert_ids.T, gate_probs.T, tokens, out_grad)
    send = send.reshape(experts * nz, rows_out, LANES)
    slot_names = jnp.arange(slots, dtype=jnp.int32)
    place0 = slot_names[:, None] == position[0][None, :]
    place1 = slot_names[:, None] == position[1][None, :]
    placing = (place0 | place1).astype(jnp.bfloat16)
    part_rows = experts * nz * CAP
    gate_w = w_gate[0]
    up_w = w_up[0]
    down_w = w_down[0]
    hid = gate_w.shape[1]

    def meet(block, mask):
        return lax.ppermute(block, "x", [(i, i ^ mask) for i in range(nx)])

    def swap(block):
        return lax.ppermute(block, "dp", [(0, 1), (1, 0)])

    def stacked(gate, up, down):
        return jnp.concatenate([gate, up] + jnp.split(down, width // hid, axis=1), axis=0)

    def unstacked(stack):
        gate, up, down = jnp.split(stack, 3, axis=0)
        return gate, up, jnp.concatenate(jnp.split(down, width // hid, axis=0), axis=1)

    gate_n, up_n, down_n = unstacked(meet(stacked(gate_w, up_w, down_w), 1))
    gate_w = jnp.concatenate([gate_w, gate_n], axis=1)
    up_w = jnp.concatenate([up_w, up_n], axis=1)
    down_w = jnp.concatenate([down_w, down_n], axis=0)

    def project(rows):
        return jnp.concatenate(
            [
                contract(rows[:, :width], gate_w, 1, 0),
                contract(rows[:, :width], up_w, 1, 0),
                contract(rows[:, width:], down_w, 1, 1),
            ],
            axis=1,
        ).astype(jnp.bfloat16)

    def pullback(partial, other):
        total = partial.astype(jnp.float32) + other.astype(jnp.float32)
        gate_pre, up_pre, d_hidden = jnp.split(total, 3, axis=1)
        sigmoid_gate = jax.nn.sigmoid(gate_pre)
        silu_gate = gate_pre * sigmoid_gate
        hidden = (silu_gate * up_pre).astype(jnp.bfloat16)
        score = jnp.sum(d_hidden * hidden.astype(jnp.float32), axis=1)
        grad_gate_pre = (
            d_hidden * up_pre * sigmoid_gate * (1.0 + gate_pre * (1.0 - sigmoid_gate))
        ).astype(jnp.bfloat16)
        grad_up_pre = (d_hidden * silu_gate).astype(jnp.bfloat16)
        input_part = (
            contract(grad_gate_pre, gate_w, 1, 1) + contract(grad_up_pre, up_w, 1, 1)
        ).astype(jnp.bfloat16)
        return hidden, grad_gate_pre, grad_up_pre, input_part, score.astype(jnp.bfloat16)

    def packed(input_part, score):
        score_row = jnp.pad(score.reshape(1, part_rows), ((0, 7), (0, width - part_rows)))
        return jnp.concatenate([input_part, score_row], axis=0)

    own = exchange(send, ("expert", "z")).reshape(part_rows, 2 * width)
    guest = meet(own, 3)
    own, guest = lax.optimization_barrier((own, guest))
    rows = jnp.concatenate([guest, own], axis=0)
    partial = project(rows)
    hidden, grad_gate_pre, grad_up_pre, input_part, score = pullback(partial, swap(partial))
    back = meet(packed(input_part[:part_rows], score[:part_rows]), 3)
    back = (
        packed(input_part[part_rows:], score[part_rows:]).astype(jnp.float32)
        + back.astype(jnp.float32)
    ).astype(jnp.bfloat16)
    rows_x, rows_dy = rows[:, :width], rows[:, width:]

    def weight_grads(part):
        return (
            contract(rows_x, grad_gate_pre[:, part], 0, 0),
            contract(rows_x, grad_up_pre[:, part], 0, 0),
            contract(hidden[:, part], rows_dy, 0, 0),
        )

    theirs = [g.astype(jnp.bfloat16) for g in weight_grads(slice(hid, None))]
    theirs = meet(stacked(*theirs), 1)
    mine = lax.optimization_barrier(weight_grads(slice(0, hid)))
    grad_gate, grad_up, grad_down = (
        (own_part + other.astype(jnp.float32)).astype(jnp.bfloat16)[None]
        for own_part, other in zip(mine, unstacked(theirs))
    )

    data = back[:part_rows].reshape(experts * nz, CAP * chunks, LANES)
    marks = jnp.pad(
        back[part_rows, :part_rows].reshape(experts * nz, 1, CAP),
        ((0, 0), (0, 1), (0, LANES - CAP)),
    )
    home = jnp.concatenate([data, marks], axis=1)
    home = exchange(
        home.reshape(experts * nz, CAP * chunks // 2 + 1, 2, LANES), ("expert", "z")
    )
    home = jnp.sum(
        home.reshape(experts, nz, CAP * chunks + 2, LANES).astype(jnp.float32), axis=1
    )
    pair_rows = home[:, : CAP * chunks].astype(jnp.bfloat16).reshape(slots, width)
    pair_score = home[:, CAP * chunks, :CAP].reshape(slots, 1)
    grad_tokens = contract(placing, pair_rows, 0, 0).astype(jnp.bfloat16)
    score0 = jnp.sum(jnp.where(place0, pair_score, 0.0), axis=0)
    score1 = jnp.sum(jnp.where(place1, pair_score, 0.0), axis=0)
    grad_probs = (jnp.stack([score0, score1], axis=1) / probs).astype(jnp.bfloat16)
    return (grad_tokens, grad_gate, grad_up, grad_down, grad_probs)


def solution(mesh):
    names = dict(zip(mesh.axis_names, mesh.devices.shape))
    nz = 8
    nx = names["ffn"] // nz
    grid = Mesh(
        mesh.devices.reshape(names["expert"], nx, nz, names["dp"]), ("expert", "x", "z", "dp")
    )
    toks = P(("expert", "x", "z"), "dp")
    pairs = P(("expert", "x", "z"), None)
    wide = P("expert", "dp", ("x", "z"))
    tall = P("expert", ("x", "z"), "dp")
    return jax.shard_map(
        per_device,
        mesh=grid,
        in_specs=(toks, toks, pairs, pairs, wide, wide, tall),
        out_specs=(toks, wide, wide, tall, pairs),
        check_vma=False,
    )
```

```python
import functools

import jax
import jax.numpy as jnp
from jax import lax
from jax.experimental import pallas as pl
from jax.experimental.pallas import tpu as pltpu
from jax.sharding import Mesh
from jax.sharding import PartitionSpec as P

CAP = 3
LANES = 128


def contract(left, right, left_dim, right_dim):
    return lax.dot_general(
        left, right, (((left_dim,), (right_dim,)), ((), ())), preferred_element_type=jnp.float32
    )


def exchange(block, axes):
    return lax.all_to_all(block, axes, split_axis=0, concat_axis=0, tiled=True)


def dispatch_kernel(ids_ref, probs_ref, tokens_ref, out_grad_ref, send_ref, position_ref, stage_ref):
    experts, nz = send_ref.shape[0], send_ref.shape[1]
    toks, width = tokens_ref.shape
    chunks = width // LANES
    ids = [ids_ref[k : k + 1, :] for k in range(2)]
    probs = [probs_ref[k : k + 1, :].astype(jnp.bfloat16).astype(jnp.float32) for k in range(2)]
    a = lax.broadcasted_iota(jnp.int32, (toks, toks), 0)
    b = lax.broadcasted_iota(jnp.int32, (toks, toks), 1)
    columns = [
        jnp.sum(jnp.where(a == b, jnp.broadcast_to(i, (toks, toks)), 0), axis=1, keepdims=True)
        for i in ids
    ]
    places = []
    for k in range(2):
        rank = jnp.zeros((1, toks), jnp.int32)
        for other in range(2):
            earlier = (a < b) if other >= k else (a <= b)
            match = (columns[other] == ids[k]) & earlier
            rank = rank + jnp.sum(match.astype(jnp.int32), axis=0, keepdims=True)
        position_ref[k : k + 1, :] = ids[k] * CAP + rank
        places.append((ids[k], rank))
    names = lax.broadcasted_iota(jnp.int32, (experts, toks), 0)
    x = tokens_ref[...].astype(jnp.float32)
    dy = out_grad_ref[...].astype(jnp.float32)
    for slot in range(CAP):
        masks = [(names == i) & (rank == slot) for i, rank in places]
        hit = (masks[0] | masks[1]).astype(jnp.float32)
        weight = jnp.sum(
            jnp.where(masks[0], probs[0], 0.0) + jnp.where(masks[1], probs[1], 0.0),
            axis=1,
            keepdims=True,
        )
        rows_x = jnp.zeros((experts, width), jnp.float32)
        rows_dy = jnp.zeros((experts, width), jnp.float32)
        for t in range(toks):
            rows_x = rows_x + hit[:, t : t + 1] * x[t : t + 1, :]
            rows_dy = rows_dy + hit[:, t : t + 1] * dy[t : t + 1, :]
        rows_dy = rows_dy * weight
        for c in range(chunks):
            lanes = slice(c * LANES, (c + 1) * LANES)
            stage_ref[:, slot * 2 * chunks + c, :] = rows_x[:, lanes]
            stage_ref[:, slot * 2 * chunks + chunks + c, :] = rows_dy[:, lanes]
    for e in range(experts):
        block = stage_ref[e].astype(jnp.bfloat16)
        for z in range(nz):
            send_ref[e, z] = block


def project_kernel(guest_ref, own_ref, gate_ref, up_ref, down_ref, stack_ref, partial_ref):
    width, hid = gate_ref.shape
    half = own_ref.shape[0]
    for h, rows_ref in enumerate((guest_ref, own_ref)):
        rows = slice(h * half, (h + 1) * half)
        x = rows_ref[:, :width]
        parts = [
            contract(x, gate_ref[...], 1, 0),
            contract(x, stack_ref[:width, :], 1, 0),
            contract(x, up_ref[...], 1, 0),
            contract(x, stack_ref[width : 2 * width, :], 1, 0),
            contract(rows_ref[:, width:], down_ref[...], 1, 1),
        ]
        total = None
        for k in range(width // hid):
            piece = contract(
                rows_ref[:, width + k * hid : width + (k + 1) * hid],
                stack_ref[2 * width + k * hid : 2 * width + (k + 1) * hid, :],
                1,
                1,
            )
            total = piece if total is None else total + piece
        parts.append(total)
        for k, part in enumerate(parts):
            partial_ref[rows, k * hid : (k + 1) * hid] = part.astype(jnp.bfloat16)


def pullback_kernel(
    partial_ref, other_ref, gate_ref, up_ref, stack_ref,
    pack_guest_ref, pack_own_ref, hidden_ref, gate_pre_ref, up_pre_ref, score_ref,
):
    width, hid = gate_ref.shape
    both = 2 * hid
    half = partial_ref.shape[0] // 2
    step = 16

    def one(i, carry):
        rows = pl.ds(pl.multiple_of(i * step, step), step)
        total = partial_ref[rows, :].astype(jnp.float32) + other_ref[rows, :].astype(jnp.float32)
        gate_pre, up_pre, d_hidden = total[:, :both], total[:, both : 2 * both], total[:, 2 * both :]
        sigmoid_gate = jax.nn.sigmoid(gate_pre)
        silu_gate = gate_pre * sigmoid_gate
        hidden = (silu_gate * up_pre).astype(jnp.bfloat16)
        score = jnp.sum(d_hidden * hidden.astype(jnp.float32), axis=1, keepdims=True)
        hidden_ref[rows, :] = hidden
        gate_pre_ref[rows, :] = (
            d_hidden * up_pre * sigmoid_gate * (1.0 + gate_pre * (1.0 - sigmoid_gate))
        ).astype(jnp.bfloat16)
        up_pre_ref[rows, :] = (d_hidden * silu_gate).astype(jnp.bfloat16)
        score_ref[rows, :] = jnp.broadcast_to(score, (step, LANES))
        return carry

    lax.fori_loop(0, partial_ref.shape[0] // step, one, 0)
    a = lax.broadcasted_iota(jnp.int32, (half, LANES), 0)
    b = lax.broadcasted_iota(jnp.int32, (half, LANES), 1)
    for h, pack_ref in enumerate((pack_guest_ref, pack_own_ref)):
        rows = slice(h * half, (h + 1) * half)
        pack_ref[:half, :] = (
            contract(gate_pre_ref[rows, :hid], gate_ref[...], 1, 1)
            + contract(gate_pre_ref[rows, hid:], stack_ref[:width, :], 1, 1)
            + contract(up_pre_ref[rows, :hid], up_ref[...], 1, 1)
            + contract(up_pre_ref[rows, hid:], stack_ref[width : 2 * width, :], 1, 1)
        ).astype(jnp.bfloat16)
        pack_ref[half:, :] = jnp.zeros((pack_ref.shape[0] - half, width), jnp.bfloat16)
        score = score_ref[rows, :]
        for k in range(-(-half // LANES)):
            row = jnp.sum(jnp.where(a == b + k * LANES, score, 0.0), axis=0, keepdims=True)
            pack_ref[half:, k * LANES : (k + 1) * LANES] = jnp.broadcast_to(
                row, (pack_ref.shape[0] - half, LANES)
            ).astype(jnp.bfloat16)


def products_kernel(guest_ref, own_ref, hidden_ref, gate_pre_ref, up_pre_ref, out_ref, *, first):
    hid = out_ref.shape[1]
    width = guest_ref.shape[1] // 2
    half = guest_ref.shape[0]
    part = slice(first, first + hid)
    step = 256

    def product(left, right):
        return sum(
            contract(left(ref, rows), right(ref, rows), 0, 0)
            for ref, rows in ((guest_ref, slice(0, half)), (own_ref, slice(half, 2 * half)))
        ).astype(out_ref.dtype)

    for k in range(width // step):
        cols = slice(k * step, (k + 1) * step)
        out_ref[cols, :] = product(lambda ref, _: ref[:, cols], lambda _, rows: gate_pre_ref[rows, part])
        out_ref[width + k * step : width + (k + 1) * step, :] = product(
            lambda ref, _: ref[:, cols], lambda _, rows: up_pre_ref[rows, part]
        )
    for k in range(width // hid):
        cols = slice(width + k * hid, width + (k + 1) * hid)
        out_ref[2 * width + k * hid : 2 * width + (k + 1) * hid, :] = product(
            lambda _, rows: hidden_ref[rows, part], lambda ref, _: ref[:, cols]
        )


def settle_kernel(mine_ref, theirs_ref, gate_ref, up_ref, down_ref):
    width, hid = gate_ref.shape[1:]

    def total(start, size):
        rows = slice(start, start + size)
        return (mine_ref[rows, :] + theirs_ref[rows, :].astype(jnp.float32)).astype(jnp.bfloat16)

    gate_ref[0] = total(0, width)
    up_ref[0] = total(width, width)
    for k in range(width // hid):
        down_ref[0, :, k * hid : (k + 1) * hid] = total(2 * width + k * hid, hid)


def per_device(tokens, out_grad, expert_ids, gate_probs, w_gate, w_up, w_down):
    experts = lax.axis_size("expert")
    nx = lax.axis_size("x")
    nz = lax.axis_size("z")
    tok_rows, width = tokens.shape
    chunks = width // LANES
    slots = experts * CAP

    probs = gate_probs.astype(jnp.bfloat16).astype(jnp.float32)
    rows_out = CAP * 2 * chunks
    send, position = pl.pallas_call(
        dispatch_kernel,
        out_shape=(
            jax.ShapeDtypeStruct((experts, nz, rows_out, LANES), jnp.bfloat16),
            jax.ShapeDtypeStruct((2, tok_rows), jnp.int32),
        ),
        in_specs=[pl.BlockSpec(memory_space=pltpu.VMEM)] * 4,
        out_specs=(
            pl.BlockSpec(memory_space=pltpu.VMEM),
            pl.BlockSpec(memory_space=pltpu.VMEM),
        ),
        scratch_shapes=[pltpu.VMEM((experts, rows_out, LANES), jnp.float32)],
    )(expert_ids.T, gate_probs.T, tokens, out_grad)
    send = send.reshape(experts * nz, rows_out, LANES)
    slot_names = jnp.arange(slots, dtype=jnp.int32)
    place0 = slot_names[:, None] == position[0][None, :]
    place1 = slot_names[:, None] == position[1][None, :]
    placing = (place0 | place1).astype(jnp.bfloat16)
    part_rows = experts * nz * CAP
    gate_w = w_gate[0]
    up_w = w_up[0]
    down_w = w_down[0]
    hid = gate_w.shape[1]

    def meet(block, mask):
        return lax.ppermute(block, "x", [(i, i ^ mask) for i in range(nx)])

    def swap(block):
        return lax.ppermute(block, "dp", [(0, 1), (1, 0)])

    def stacked(gate, up, down):
        return jnp.concatenate([gate, up] + jnp.split(down, width // hid, axis=1), axis=0)

    weights = meet(stacked(gate_w, up_w, down_w), 1)
    own = exchange(send, ("expert", "z")).reshape(part_rows, 2 * width)
    guest = meet(own, 3)
    own, guest = lax.optimization_barrier((own, guest))

    vmem = pl.BlockSpec(memory_space=pltpu.VMEM)
    params = pltpu.CompilerParams(vmem_limit_bytes=40 * 1024 * 1024)

    def call(kernel, outs, args, scratch=(), flops=0):
        return pl.pallas_call(
            kernel,
            out_shape=tuple(jax.ShapeDtypeStruct(s, d) for s, d in outs),
            in_specs=[vmem] * len(args),
            out_specs=tuple(vmem for _ in outs),
            scratch_shapes=list(scratch),
            compiler_params=params,
            cost_estimate=pl.CostEstimate(flops=flops, bytes_accessed=6 << 20, transcendentals=0),
        )(*args)

    bf16 = jnp.bfloat16
    all_rows, both = 2 * part_rows, 2 * hid
    dot_flops = 2 * all_rows * width * both
    (partial,) = call(
        project_kernel,
        [((all_rows, 3 * both), bf16)],
        (guest, own, gate_w, up_w, down_w, weights),
        flops=3 * dot_flops,
    )
    pack_rows = part_rows + 16
    pack_guest, pack_own, hidden, grad_gate_pre, grad_up_pre = call(
        pullback_kernel,
        [((pack_rows, width), bf16)] * 2 + [((all_rows, both), bf16)] * 3,
        (partial, swap(partial), gate_w, up_w, weights),
        [pltpu.VMEM((all_rows, LANES), jnp.float32)],
        flops=2 * dot_flops,
    )
    back = meet(pack_guest, 3)
    terms = (guest, own, hidden, grad_gate_pre, grad_up_pre)
    (theirs,) = call(
        functools.partial(products_kernel, first=hid),
        [((3 * width, hid), bf16)],
        terms,
        flops=3 * dot_flops // 2,
    )
    theirs = meet(theirs, 1)
    back = (pack_own.astype(jnp.float32) + back.astype(jnp.float32)).astype(bf16)
    (mine,) = call(
        functools.partial(products_kernel, first=0),
        [((3 * width, hid), jnp.float32)],
        terms,
        flops=3 * dot_flops // 2,
    )
    grad_gate, grad_up, grad_down = call(
        settle_kernel,
        [((1, width, hid), bf16), ((1, width, hid), bf16), ((1, hid, width), bf16)],
        (mine, theirs),
    )

    data = back[:part_rows].reshape(experts * nz, CAP * chunks, LANES)
    marks = jnp.pad(
        back[part_rows, :part_rows].reshape(experts * nz, 1, CAP),
        ((0, 0), (0, 1), (0, LANES - CAP)),
    )
    home = jnp.concatenate([data, marks], axis=1)
    home = exchange(
        home.reshape(experts * nz, CAP * chunks // 2 + 1, 2, LANES), ("expert", "z")
    )
    home = jnp.sum(
        home.reshape(experts, nz, CAP * chunks + 2, LANES).astype(jnp.float32), axis=1
    )
    pair_rows = home[:, : CAP * chunks].astype(jnp.bfloat16).reshape(slots, width)
    pair_score = home[:, CAP * chunks, :CAP].reshape(slots, 1)
    grad_tokens = contract(placing, pair_rows, 0, 0).astype(jnp.bfloat16)
    score0 = jnp.sum(jnp.where(place0, pair_score, 0.0), axis=0)
    score1 = jnp.sum(jnp.where(place1, pair_score, 0.0), axis=0)
    grad_probs = (jnp.stack([score0, score1], axis=1) / probs).astype(jnp.bfloat16)
    return (grad_tokens, grad_gate, grad_up, grad_down, grad_probs)


def solution(mesh):
    names = dict(zip(mesh.axis_names, mesh.devices.shape))
    nz = 8
    nx = names["ffn"] // nz
    grid = Mesh(
        mesh.devices.reshape(names["expert"], nx, nz, names["dp"]), ("expert", "x", "z", "dp")
    )
    toks = P(("expert", "x", "z"), "dp")
    pairs = P(("expert", "x", "z"), None)
    wide = P("expert", "dp", ("x", "z"))
    tall = P("expert", ("x", "z"), "dp")
    return jax.shard_map(
        per_device,
        mesh=grid,
        in_specs=(toks, toks, pairs, pairs, wide, wide, tall),
        out_specs=(toks, wide, wide, tall, pairs),
        check_vma=False,
    )
```

```python
import functools

import jax
import jax.numpy as jnp
from jax import lax
from jax.experimental import pallas as pl
from jax.experimental.pallas import tpu as pltpu
from jax.sharding import Mesh
from jax.sharding import PartitionSpec as P

CAP = 3
LANES = 128


def contract(left, right, left_dim, right_dim):
    return lax.dot_general(
        left, right, (((left_dim,), (right_dim,)), ((), ())), preferred_element_type=jnp.float32
    )


def exchange(block, axes):
    return lax.all_to_all(block, axes, split_axis=0, concat_axis=0, tiled=True)


def dispatch_kernel(ids_ref, probs_ref, tokens_ref, out_grad_ref, send_ref, position_ref, stage_ref):
    experts, nz = send_ref.shape[0], send_ref.shape[1]
    toks, width = tokens_ref.shape
    chunks = width // LANES
    ids = [ids_ref[k : k + 1, :] for k in range(2)]
    probs = [probs_ref[k : k + 1, :].astype(jnp.bfloat16).astype(jnp.float32) for k in range(2)]
    a = lax.broadcasted_iota(jnp.int32, (toks, toks), 0)
    b = lax.broadcasted_iota(jnp.int32, (toks, toks), 1)
    columns = [
        jnp.sum(jnp.where(a == b, jnp.broadcast_to(i, (toks, toks)), 0), axis=1, keepdims=True)
        for i in ids
    ]
    places = []
    for k in range(2):
        rank = jnp.zeros((1, toks), jnp.int32)
        for other in range(2):
            earlier = (a < b) if other >= k else (a <= b)
            match = (columns[other] == ids[k]) & earlier
            rank = rank + jnp.sum(match.astype(jnp.int32), axis=0, keepdims=True)
        position_ref[k : k + 1, :] = ids[k] * CAP + rank
        places.append((ids[k], rank))
    names = lax.broadcasted_iota(jnp.int32, (experts, toks), 0)
    x = tokens_ref[...].astype(jnp.float32)
    dy = out_grad_ref[...].astype(jnp.float32)
    for slot in range(CAP):
        masks = [(names == i) & (rank == slot) for i, rank in places]
        hit = (masks[0] | masks[1]).astype(jnp.float32)
        weight = jnp.sum(
            jnp.where(masks[0], probs[0], 0.0) + jnp.where(masks[1], probs[1], 0.0),
            axis=1,
            keepdims=True,
        )
        rows_x = jnp.zeros((experts, width), jnp.float32)
        rows_dy = jnp.zeros((experts, width), jnp.float32)
        for t in range(toks):
            rows_x = rows_x + hit[:, t : t + 1] * x[t : t + 1, :]
            rows_dy = rows_dy + hit[:, t : t + 1] * dy[t : t + 1, :]
        rows_dy = rows_dy * weight
        for c in range(chunks):
            lanes = slice(c * LANES, (c + 1) * LANES)
            stage_ref[:, slot * 2 * chunks + c, :] = rows_x[:, lanes]
            stage_ref[:, slot * 2 * chunks + chunks + c, :] = rows_dy[:, lanes]
    for e in range(experts):
        block = stage_ref[e].astype(jnp.bfloat16)
        for z in range(nz):
            send_ref[e, z] = block


def project_kernel(guest_ref, own_ref, gate_ref, up_ref, down_ref, stack_ref, partial_ref):
    width, hid = gate_ref.shape
    half = own_ref.shape[0]
    for h, rows_ref in enumerate((guest_ref, own_ref)):
        rows = slice(h * half, (h + 1) * half)
        x = rows_ref[:, :width]
        parts = [
            contract(x, gate_ref[...], 1, 0),
            contract(x, stack_ref[:width, :], 1, 0),
            contract(x, up_ref[...], 1, 0),
            contract(x, stack_ref[width : 2 * width, :], 1, 0),
            contract(rows_ref[:, width:], down_ref[...], 1, 1),
        ]
        total = None
        for k in range(width // hid):
            piece = contract(
                rows_ref[:, width + k * hid : width + (k + 1) * hid],
                stack_ref[2 * width + k * hid : 2 * width + (k + 1) * hid, :],
                1,
                1,
            )
            total = piece if total is None else total + piece
        parts.append(total)
        for k, part in enumerate(parts):
            partial_ref[rows, k * hid : (k + 1) * hid] = part.astype(jnp.bfloat16)


def pullback_kernel(
    partial_ref, other_ref, gate_ref, up_ref, stack_ref,
    pack_ref, hidden_ref, gate_pre_ref, up_pre_ref, score_ref, *, first
):
    width, hid = gate_ref.shape
    both = 2 * hid
    half = hidden_ref.shape[0]
    step = 16

    def one(i, carry):
        rows = pl.ds(pl.multiple_of(i * step, step), step)
        source = pl.ds(pl.multiple_of(first + i * step, step), step)
        total = partial_ref[source, :].astype(jnp.float32) + other_ref[source, :].astype(jnp.float32)
        gate_pre, up_pre, d_hidden = total[:, :both], total[:, both : 2 * both], total[:, 2 * both :]
        sigmoid_gate = jax.nn.sigmoid(gate_pre)
        silu_gate = gate_pre * sigmoid_gate
        hidden = (silu_gate * up_pre).astype(jnp.bfloat16)
        score = jnp.sum(d_hidden * hidden.astype(jnp.float32), axis=1, keepdims=True)
        hidden_ref[rows, :] = hidden
        gate_pre_ref[rows, :] = (
            d_hidden * up_pre * sigmoid_gate * (1.0 + gate_pre * (1.0 - sigmoid_gate))
        ).astype(jnp.bfloat16)
        up_pre_ref[rows, :] = (d_hidden * silu_gate).astype(jnp.bfloat16)
        score_ref[rows, :] = jnp.broadcast_to(score, (step, LANES))
        return carry

    lax.fori_loop(0, half // step, one, 0)
    pack_ref[:half, :] = (
        contract(gate_pre_ref[:, :hid], gate_ref[...], 1, 1)
        + contract(gate_pre_ref[:, hid:], stack_ref[:width, :], 1, 1)
        + contract(up_pre_ref[:, :hid], up_ref[...], 1, 1)
        + contract(up_pre_ref[:, hid:], stack_ref[width : 2 * width, :], 1, 1)
    ).astype(jnp.bfloat16)
    extra = pack_ref.shape[0] - half
    pack_ref[half:, :] = jnp.zeros((extra, width), jnp.bfloat16)
    score = score_ref[...]
    a = lax.broadcasted_iota(jnp.int32, (half, LANES), 0)
    b = lax.broadcasted_iota(jnp.int32, (half, LANES), 1)
    for k in range(-(-half // LANES)):
        row = jnp.sum(jnp.where(a == b + k * LANES, score, 0.0), axis=0, keepdims=True)
        pack_ref[half:, k * LANES : (k + 1) * LANES] = jnp.broadcast_to(
            row, (extra, LANES)
        ).astype(jnp.bfloat16)


def products_kernel(*refs, first):
    out_ref = refs[-1]
    groups = (refs[:4], refs[4:8])
    hid = out_ref.shape[1]
    width = refs[0].shape[1] // 2
    part = slice(first, first + hid)

    def product(left, right):
        return sum(contract(left(group), right(group), 0, 0) for group in groups).astype(out_ref.dtype)

    for k in range(width // hid):
        low, high = k * hid, (k + 1) * hid
        out_ref[low:high, :] = product(lambda g: g[0][:, low:high], lambda g: g[2][:, part])
        out_ref[width + low : width + high, :] = product(
            lambda g: g[0][:, low:high], lambda g: g[3][:, part]
        )
        out_ref[2 * width + low : 2 * width + high, :] = product(
            lambda g: g[1][:, part], lambda g: g[0][:, width + low : width + high]
        )


def settle_kernel(mine_ref, theirs_ref, gate_ref, up_ref, down_ref):
    width, hid = gate_ref.shape[1:]

    def total(start, size):
        rows = slice(start, start + size)
        return (mine_ref[rows, :] + theirs_ref[rows, :].astype(jnp.float32)).astype(jnp.bfloat16)

    gate_ref[0] = total(0, width)
    up_ref[0] = total(width, width)
    for k in range(width // hid):
        down_ref[0, :, k * hid : (k + 1) * hid] = total(2 * width + k * hid, hid)


def per_device(tokens, out_grad, expert_ids, gate_probs, w_gate, w_up, w_down):
    experts = lax.axis_size("expert")
    nx = lax.axis_size("x")
    nz = lax.axis_size("z")
    tok_rows, width = tokens.shape
    chunks = width // LANES
    slots = experts * CAP

    probs = gate_probs.astype(jnp.bfloat16).astype(jnp.float32)
    rows_out = CAP * 2 * chunks
    send, position = pl.pallas_call(
        dispatch_kernel,
        out_shape=(
            jax.ShapeDtypeStruct((experts, nz, rows_out, LANES), jnp.bfloat16),
            jax.ShapeDtypeStruct((2, tok_rows), jnp.int32),
        ),
        in_specs=[pl.BlockSpec(memory_space=pltpu.VMEM)] * 4,
        out_specs=(
            pl.BlockSpec(memory_space=pltpu.VMEM),
            pl.BlockSpec(memory_space=pltpu.VMEM),
        ),
        scratch_shapes=[pltpu.VMEM((experts, rows_out, LANES), jnp.float32)],
        compiler_params=pltpu.CompilerParams(vmem_limit_bytes=40 << 20),
    )(expert_ids.T, gate_probs.T, tokens, out_grad)
    send = send.reshape(experts * nz, rows_out, LANES)
    slot_names = jnp.arange(slots, dtype=jnp.int32)
    place0 = slot_names[:, None] == position[0][None, :]
    place1 = slot_names[:, None] == position[1][None, :]
    placing = (place0 | place1).astype(jnp.bfloat16)
    part_rows = experts * nz * CAP
    gate_w = w_gate[0]
    up_w = w_up[0]
    down_w = w_down[0]
    hid = gate_w.shape[1]

    def meet(block, mask):
        return lax.ppermute(block, "x", [(i, i ^ mask) for i in range(nx)])

    def swap(block):
        return lax.ppermute(block, "dp", [(0, 1), (1, 0)])

    def stacked(gate, up, down):
        return jnp.concatenate([gate, up] + jnp.split(down, width // hid, axis=1), axis=0)

    weights = meet(stacked(gate_w, up_w, down_w), 1)
    own = exchange(send, ("expert", "z")).reshape(part_rows, 2 * width)
    guest = meet(own, 3)
    own, guest = lax.optimization_barrier((own, guest))

    vmem = pl.BlockSpec(memory_space=pltpu.VMEM)
    params = pltpu.CompilerParams(vmem_limit_bytes=16 << 20)

    def call(kernel, outs, args, scratch=(), flops=0):
        return pl.pallas_call(
            kernel,
            out_shape=tuple(jax.ShapeDtypeStruct(s, d) for s, d in outs),
            in_specs=[vmem] * len(args),
            out_specs=tuple(vmem for _ in outs),
            scratch_shapes=list(scratch),
            compiler_params=params,
            cost_estimate=pl.CostEstimate(flops=flops, bytes_accessed=6 << 20, transcendentals=0),
        )(*args)

    bf16 = jnp.bfloat16
    all_rows, both = 2 * part_rows, 2 * hid
    dot_flops = 2 * all_rows * width * both
    (partial,) = call(
        project_kernel,
        [((all_rows, 3 * both), bf16)],
        (guest, own, gate_w, up_w, down_w, weights),
        flops=3 * dot_flops,
    )
    pack_rows = part_rows + 16
    other = swap(partial)

    def pulled(first):
        return call(
            functools.partial(pullback_kernel, first=first),
            [((pack_rows, width), bf16)] + [((part_rows, both), bf16)] * 3,
            (partial, other, gate_w, up_w, weights),
            [pltpu.VMEM((part_rows, LANES), jnp.float32)],
            flops=dot_flops,
        )

    pack_guest, *terms_guest = pulled(0)
    back = meet(pack_guest, 3)
    pack_own, *terms_own = pulled(part_rows)
    terms = (guest, *terms_guest, own, *terms_own)
    (theirs,) = call(
        functools.partial(products_kernel, first=hid),
        [((3 * width, hid), bf16)],
        terms,
        flops=3 * dot_flops // 2,
    )
    theirs = meet(theirs, 1)
    back = (pack_own.astype(jnp.float32) + back.astype(jnp.float32)).astype(bf16)
    (mine,) = call(
        functools.partial(products_kernel, first=0),
        [((3 * width, hid), jnp.float32)],
        terms,
        flops=3 * dot_flops // 2,
    )
    grad_gate, grad_up, grad_down = call(
        settle_kernel,
        [((1, width, hid), bf16), ((1, width, hid), bf16), ((1, hid, width), bf16)],
        (mine, theirs),
    )

    data = back[:part_rows].reshape(experts * nz, CAP * chunks, LANES)
    marks = jnp.pad(
        back[part_rows, :part_rows].reshape(experts * nz, 1, CAP),
        ((0, 0), (0, 1), (0, LANES - CAP)),
    )
    home = jnp.concatenate([data, marks], axis=1)
    home = exchange(
        home.reshape(experts * nz, CAP * chunks // 2 + 1, 2, LANES), ("expert", "z")
    )
    home = jnp.sum(
        home.reshape(experts, nz, CAP * chunks + 2, LANES).astype(jnp.float32), axis=1
    )
    pair_rows = home[:, : CAP * chunks].astype(jnp.bfloat16).reshape(slots, width)
    pair_score = home[:, CAP * chunks, :CAP].reshape(slots, 1)
    grad_tokens = contract(placing, pair_rows, 0, 0).astype(jnp.bfloat16)
    score0 = jnp.sum(jnp.where(place0, pair_score, 0.0), axis=0)
    score1 = jnp.sum(jnp.where(place1, pair_score, 0.0), axis=0)
    grad_probs = (jnp.stack([score0, score1], axis=1) / probs).astype(jnp.bfloat16)
    return (grad_tokens, grad_gate, grad_up, grad_down, grad_probs)


def solution(mesh):
    names = dict(zip(mesh.axis_names, mesh.devices.shape))
    nz = 8
    nx = names["ffn"] // nz
    grid = Mesh(
        mesh.devices.reshape(names["expert"], nx, nz, names["dp"]), ("expert", "x", "z", "dp")
    )
    toks = P(("expert", "x", "z"), "dp")
    pairs = P(("expert", "x", "z"), None)
    wide = P("expert", "dp", ("x", "z"))
    tall = P("expert", ("x", "z"), "dp")
    return jax.shard_map(
        per_device,
        mesh=grid,
        in_specs=(toks, toks, pairs, pairs, wide, wide, tall),
        out_specs=(toks, wide, wide, tall, pairs),
        check_vma=False,
    )
```

```python
import functools

import jax
import jax.numpy as jnp
from jax import lax
from jax.experimental import pallas as pl
from jax.experimental.pallas import tpu as pltpu
from jax.sharding import Mesh
from jax.sharding import PartitionSpec as P

CAP = 3
LANES = 128


def contract(left, right, left_dim, right_dim):
    return lax.dot_general(
        left, right, (((left_dim,), (right_dim,)), ((), ())), preferred_element_type=jnp.float32
    )


def exchange(block, axes):
    return lax.all_to_all(block, axes, split_axis=0, concat_axis=0, tiled=True)


def dispatch_kernel(ids_ref, probs_ref, tokens_ref, out_grad_ref, send_ref, position_ref, stage_ref):
    experts, nz = send_ref.shape[0], send_ref.shape[1]
    toks, width = tokens_ref.shape
    chunks = width // LANES
    ids = [ids_ref[k : k + 1, :] for k in range(2)]
    probs = [probs_ref[k : k + 1, :].astype(jnp.bfloat16).astype(jnp.float32) for k in range(2)]
    a = lax.broadcasted_iota(jnp.int32, (toks, toks), 0)
    b = lax.broadcasted_iota(jnp.int32, (toks, toks), 1)
    columns = [
        jnp.sum(jnp.where(a == b, jnp.broadcast_to(i, (toks, toks)), 0), axis=1, keepdims=True)
        for i in ids
    ]
    places = []
    for k in range(2):
        rank = jnp.zeros((1, toks), jnp.int32)
        for other in range(2):
            earlier = (a < b) if other >= k else (a <= b)
            match = (columns[other] == ids[k]) & earlier
            rank = rank + jnp.sum(match.astype(jnp.int32), axis=0, keepdims=True)
        position_ref[k : k + 1, :] = ids[k] * CAP + rank
        places.append((ids[k], rank))
    names = lax.broadcasted_iota(jnp.int32, (experts, toks), 0)
    x = tokens_ref[...].astype(jnp.float32)
    dy = out_grad_ref[...].astype(jnp.float32)
    for slot in range(CAP):
        masks = [(names == i) & (rank == slot) for i, rank in places]
        hit = (masks[0] | masks[1]).astype(jnp.float32)
        weight = jnp.sum(
            jnp.where(masks[0], probs[0], 0.0) + jnp.where(masks[1], probs[1], 0.0),
            axis=1,
            keepdims=True,
        )
        rows_x = jnp.zeros((experts, width), jnp.float32)
        rows_dy = jnp.zeros((experts, width), jnp.float32)
        for t in range(toks):
            rows_x = rows_x + hit[:, t : t + 1] * x[t : t + 1, :]
            rows_dy = rows_dy + hit[:, t : t + 1] * dy[t : t + 1, :]
        rows_dy = rows_dy * weight
        for c in range(chunks):
            lanes = slice(c * LANES, (c + 1) * LANES)
            stage_ref[:, slot * 2 * chunks + c, :] = rows_x[:, lanes]
            stage_ref[:, slot * 2 * chunks + chunks + c, :] = rows_dy[:, lanes]
    for e in range(experts):
        block = stage_ref[e].astype(jnp.bfloat16)
        for z in range(nz):
            send_ref[e, z] = block


def project_kernel(guest_ref, own_ref, gate_ref, up_ref, down_ref, stack_ref, partial_ref):
    width, hid = gate_ref.shape
    half = own_ref.shape[0]
    for h, rows_ref in enumerate((guest_ref, own_ref)):
        rows = slice(h * half, (h + 1) * half)
        x = rows_ref[:, :width]
        parts = [
            contract(x, gate_ref[...], 1, 0),
            contract(x, stack_ref[:width, :], 1, 0),
            contract(x, up_ref[...], 1, 0),
            contract(x, stack_ref[width : 2 * width, :], 1, 0),
            contract(rows_ref[:, width:], down_ref[...], 1, 1),
        ]
        total = None
        for k in range(width // hid):
            piece = contract(
                rows_ref[:, width + k * hid : width + (k + 1) * hid],
                stack_ref[2 * width + k * hid : 2 * width + (k + 1) * hid, :],
                1,
                1,
            )
            total = piece if total is None else total + piece
        parts.append(total)
        for k, part in enumerate(parts):
            partial_ref[rows, k * hid : (k + 1) * hid] = part.astype(jnp.bfloat16)


def pullback_kernel(
    partial_ref, other_ref, gate_ref, up_ref, stack_ref,
    pack_ref, hidden_ref, gate_pre_ref, up_pre_ref, score_ref, *, first
):
    width, hid = gate_ref.shape
    both = 2 * hid
    half = hidden_ref.shape[0]
    step = 16

    def one(i, carry):
        rows = pl.ds(pl.multiple_of(i * step, step), step)
        source = pl.ds(pl.multiple_of(first + i * step, step), step)
        total = partial_ref[source, :].astype(jnp.float32) + other_ref[source, :].astype(jnp.float32)
        gate_pre, up_pre, d_hidden = total[:, :both], total[:, both : 2 * both], total[:, 2 * both :]
        sigmoid_gate = jax.nn.sigmoid(gate_pre)
        silu_gate = gate_pre * sigmoid_gate
        hidden = (silu_gate * up_pre).astype(jnp.bfloat16)
        score = jnp.sum(d_hidden * hidden.astype(jnp.float32), axis=1, keepdims=True)
        hidden_ref[rows, :] = hidden
        gate_pre_ref[rows, :] = (
            d_hidden * up_pre * sigmoid_gate * (1.0 + gate_pre * (1.0 - sigmoid_gate))
        ).astype(jnp.bfloat16)
        up_pre_ref[rows, :] = (d_hidden * silu_gate).astype(jnp.bfloat16)
        score_ref[rows, :] = jnp.broadcast_to(score, (step, LANES))
        return carry

    lax.fori_loop(0, half // step, one, 0)
    pack_ref[:half, :] = (
        contract(gate_pre_ref[:, :hid], gate_ref[...], 1, 1)
        + contract(gate_pre_ref[:, hid:], stack_ref[:width, :], 1, 1)
        + contract(up_pre_ref[:, :hid], up_ref[...], 1, 1)
        + contract(up_pre_ref[:, hid:], stack_ref[width : 2 * width, :], 1, 1)
    ).astype(jnp.bfloat16)
    extra = pack_ref.shape[0] - half
    pack_ref[half:, :] = jnp.zeros((extra, width), jnp.bfloat16)
    score = score_ref[...]
    a = lax.broadcasted_iota(jnp.int32, (half, LANES), 0)
    b = lax.broadcasted_iota(jnp.int32, (half, LANES), 1)
    for k in range(-(-half // LANES)):
        row = jnp.sum(jnp.where(a == b + k * LANES, score, 0.0), axis=0, keepdims=True)
        pack_ref[half:, k * LANES : (k + 1) * LANES] = jnp.broadcast_to(
            row, (extra, LANES)
        ).astype(jnp.bfloat16)


def products_kernel(*refs, first):
    out_ref = refs[-1]
    groups = (refs[:4], refs[4:8])
    hid = out_ref.shape[1]
    width = refs[0].shape[1] // 2
    part = slice(first, first + hid)

    def product(left, right):
        return sum(contract(left(group), right(group), 0, 0) for group in groups).astype(out_ref.dtype)

    for k in range(width // hid):
        low, high = k * hid, (k + 1) * hid
        out_ref[low:high, :] = product(lambda g: g[0][:, low:high], lambda g: g[2][:, part])
        out_ref[width + low : width + high, :] = product(
            lambda g: g[0][:, low:high], lambda g: g[3][:, part]
        )
        out_ref[2 * width + low : 2 * width + high, :] = product(
            lambda g: g[1][:, part], lambda g: g[0][:, width + low : width + high]
        )


def settle_kernel(
    mine_ref, theirs_hbm, gate_hbm, up_hbm, down_hbm, theirs_ref, wide_ref, tall_ref, in_sem, out_sem
):
    width, hid = gate_hbm.shape[1:]
    loads = []
    for k in range(3):
        rows = pl.ds(k * width, width)
        loads.append(
            pltpu.make_async_copy(theirs_hbm.at[rows, :], theirs_ref.at[rows, :], in_sem.at[k])
        )
        loads[-1].start()

    def total(start, size):
        rows = slice(start, start + size)
        return (mine_ref[rows, :] + theirs_ref[rows, :].astype(jnp.float32)).astype(jnp.bfloat16)

    stores = []
    for k, out in enumerate((gate_hbm, up_hbm)):
        loads[k].wait()
        wide_ref[k] = total(k * width, width)
        stores.append(pltpu.make_async_copy(wide_ref.at[k], out.at[0], out_sem.at[k]))
        stores[-1].start()
    loads[2].wait()
    for k in range(width // hid):
        tall_ref[:, k * hid : (k + 1) * hid] = total(2 * width + k * hid, hid)
    stores.append(pltpu.make_async_copy(tall_ref, down_hbm.at[0], out_sem.at[2]))
    stores[-1].start()
    for store in stores:
        store.wait()


def per_device(tokens, out_grad, expert_ids, gate_probs, w_gate, w_up, w_down):
    experts = lax.axis_size("expert")
    nx = lax.axis_size("x")
    nz = lax.axis_size("z")
    tok_rows, width = tokens.shape
    chunks = width // LANES
    slots = experts * CAP

    probs = gate_probs.astype(jnp.bfloat16).astype(jnp.float32)
    rows_out = CAP * 2 * chunks
    send, position = pl.pallas_call(
        dispatch_kernel,
        out_shape=(
            jax.ShapeDtypeStruct((experts, nz, rows_out, LANES), jnp.bfloat16),
            jax.ShapeDtypeStruct((2, tok_rows), jnp.int32),
        ),
        in_specs=[pl.BlockSpec(memory_space=pltpu.VMEM)] * 4,
        out_specs=(
            pl.BlockSpec(memory_space=pltpu.VMEM),
            pl.BlockSpec(memory_space=pltpu.VMEM),
        ),
        scratch_shapes=[pltpu.VMEM((experts, rows_out, LANES), jnp.float32)],
    )(expert_ids.T, gate_probs.T, tokens, out_grad)
    send = send.reshape(experts * nz, rows_out, LANES)
    slot_names = jnp.arange(slots, dtype=jnp.int32)
    place0 = slot_names[:, None] == position[0][None, :]
    place1 = slot_names[:, None] == position[1][None, :]
    placing = (place0 | place1).astype(jnp.bfloat16)
    part_rows = experts * nz * CAP
    gate_w = w_gate[0]
    up_w = w_up[0]
    down_w = w_down[0]
    hid = gate_w.shape[1]

    def meet(block, mask):
        return lax.ppermute(block, "x", [(i, i ^ mask) for i in range(nx)])

    def swap(block):
        return lax.ppermute(block, "dp", [(0, 1), (1, 0)])

    def stacked(gate, up, down):
        return jnp.concatenate([gate, up] + jnp.split(down, width // hid, axis=1), axis=0)

    weights = meet(stacked(gate_w, up_w, down_w), 1)
    own = exchange(send, ("expert", "z")).reshape(part_rows, 2 * width)
    guest = meet(own, 3)
    own, guest = lax.optimization_barrier((own, guest))

    vmem = pl.BlockSpec(memory_space=pltpu.VMEM)
    params = pltpu.CompilerParams(vmem_limit_bytes=16 << 20)

    hbm = pl.BlockSpec(memory_space=pl.ANY)

    def call(kernel, outs, args, scratch=(), flops=0, far=(), far_out=False):
        return pl.pallas_call(
            kernel,
            out_shape=tuple(jax.ShapeDtypeStruct(s, d) for s, d in outs),
            in_specs=[hbm if k in far else vmem for k in range(len(args))],
            out_specs=tuple(hbm if far_out else vmem for _ in outs),
            scratch_shapes=list(scratch),
            compiler_params=params,
            cost_estimate=pl.CostEstimate(flops=flops, bytes_accessed=6 << 20, transcendentals=0),
        )(*args)

    bf16 = jnp.bfloat16
    all_rows, both = 2 * part_rows, 2 * hid
    dot_flops = 2 * all_rows * width * both
    (partial,) = call(
        project_kernel,
        [((all_rows, 3 * both), bf16)],
        (guest, own, gate_w, up_w, down_w, weights),
        flops=3 * dot_flops,
    )
    pack_rows = part_rows + 16
    other = swap(partial)

    def pulled(first):
        return call(
            functools.partial(pullback_kernel, first=first),
            [((pack_rows, width), bf16)] + [((part_rows, both), bf16)] * 3,
            (partial, other, gate_w, up_w, weights),
            [pltpu.VMEM((part_rows, LANES), jnp.float32)],
            flops=dot_flops,
        )

    pack_guest, *terms_guest = pulled(0)
    back = meet(pack_guest, 3)
    pack_own, *terms_own = pulled(part_rows)
    terms = (guest, *terms_guest, own, *terms_own)
    (theirs,) = call(
        functools.partial(products_kernel, first=hid),
        [((3 * width, hid), bf16)],
        terms,
        flops=3 * dot_flops // 2,
    )
    theirs = meet(theirs, 1)
    back = (pack_own.astype(jnp.float32) + back.astype(jnp.float32)).astype(bf16)
    (mine,) = call(
        functools.partial(products_kernel, first=0),
        [((3 * width, hid), jnp.float32)],
        terms,
        flops=3 * dot_flops // 2,
    )
    grad_gate, grad_up, grad_down = call(
        settle_kernel,
        [((1, width, hid), bf16), ((1, width, hid), bf16), ((1, hid, width), bf16)],
        (mine, theirs),
        [
            pltpu.VMEM((3 * width, hid), bf16),
            pltpu.VMEM((2, width, hid), bf16),
            pltpu.VMEM((hid, width), bf16),
            pltpu.SemaphoreType.DMA((3,)),
            pltpu.SemaphoreType.DMA((3,)),
        ],
        far=(1,),
        far_out=True,
    )

    data = back[:part_rows].reshape(experts * nz, CAP * chunks, LANES)
    marks = jnp.pad(
        back[part_rows, :part_rows].reshape(experts * nz, 1, CAP),
        ((0, 0), (0, 1), (0, LANES - CAP)),
    )
    home = jnp.concatenate([data, marks], axis=1)
    home = exchange(
        home.reshape(experts * nz, CAP * chunks // 2 + 1, 2, LANES), ("expert", "z")
    )
    home = jnp.sum(
        home.reshape(experts, nz, CAP * chunks + 2, LANES).astype(jnp.float32), axis=1
    )
    pair_rows = home[:, : CAP * chunks].astype(jnp.bfloat16).reshape(slots, width)
    pair_score = home[:, CAP * chunks, :CAP].reshape(slots, 1)
    grad_tokens = contract(placing, pair_rows, 0, 0).astype(jnp.bfloat16)
    score0 = jnp.sum(jnp.where(place0, pair_score, 0.0), axis=0)
    score1 = jnp.sum(jnp.where(place1, pair_score, 0.0), axis=0)
    grad_probs = (jnp.stack([score0, score1], axis=1) / probs).astype(jnp.bfloat16)
    return (grad_tokens, grad_gate, grad_up, grad_down, grad_probs)


def solution(mesh):
    names = dict(zip(mesh.axis_names, mesh.devices.shape))
    nz = 8
    nx = names["ffn"] // nz
    grid = Mesh(
        mesh.devices.reshape(names["expert"], nx, nz, names["dp"]), ("expert", "x", "z", "dp")
    )
    toks = P(("expert", "x", "z"), "dp")
    pairs = P(("expert", "x", "z"), None)
    wide = P("expert", "dp", ("x", "z"))
    tall = P("expert", ("x", "z"), "dp")
    return jax.shard_map(
        per_device,
        mesh=grid,
        in_specs=(toks, toks, pairs, pairs, wide, wide, tall),
        out_specs=(toks, wide, wide, tall, pairs),
        check_vma=False,
    )
```

```python
import functools

import jax
import jax.numpy as jnp
from jax import lax
from jax.experimental import pallas as pl
from jax.experimental.pallas import tpu as pltpu
from jax.sharding import Mesh
from jax.sharding import PartitionSpec as P

CAP = 3
LANES = 128


def contract(left, right, left_dim, right_dim):
    return lax.dot_general(
        left, right, (((left_dim,), (right_dim,)), ((), ())), preferred_element_type=jnp.float32
    )


def exchange(block, axes):
    return lax.all_to_all(block, axes, split_axis=0, concat_axis=0, tiled=True)


def dispatch_kernel(ids_ref, probs_ref, tokens_ref, out_grad_ref, send_ref, position_ref, stage_ref):
    experts, nz = send_ref.shape[0], send_ref.shape[1]
    toks, width = tokens_ref.shape
    chunks = width // LANES
    ids = [ids_ref[k : k + 1, :] for k in range(2)]
    probs = [probs_ref[k : k + 1, :].astype(jnp.bfloat16).astype(jnp.float32) for k in range(2)]
    a = lax.broadcasted_iota(jnp.int32, (toks, toks), 0)
    b = lax.broadcasted_iota(jnp.int32, (toks, toks), 1)
    columns = [
        jnp.sum(jnp.where(a == b, jnp.broadcast_to(i, (toks, toks)), 0), axis=1, keepdims=True)
        for i in ids
    ]
    places = []
    for k in range(2):
        rank = jnp.zeros((1, toks), jnp.int32)
        for other in range(2):
            earlier = (a < b) if other >= k else (a <= b)
            match = (columns[other] == ids[k]) & earlier
            rank = rank + jnp.sum(match.astype(jnp.int32), axis=0, keepdims=True)
        position_ref[k : k + 1, :] = ids[k] * CAP + rank
        places.append((ids[k], rank))
    names = lax.broadcasted_iota(jnp.int32, (experts, toks), 0)
    x = tokens_ref[...].astype(jnp.float32)
    dy = out_grad_ref[...].astype(jnp.float32)
    for slot in range(CAP):
        masks = [(names == i) & (rank == slot) for i, rank in places]
        hit = (masks[0] | masks[1]).astype(jnp.float32)
        weight = jnp.sum(
            jnp.where(masks[0], probs[0], 0.0) + jnp.where(masks[1], probs[1], 0.0),
            axis=1,
            keepdims=True,
        )
        rows_x = jnp.zeros((experts, width), jnp.float32)
        rows_dy = jnp.zeros((experts, width), jnp.float32)
        for t in range(toks):
            rows_x = rows_x + hit[:, t : t + 1] * x[t : t + 1, :]
            rows_dy = rows_dy + hit[:, t : t + 1] * dy[t : t + 1, :]
        rows_dy = rows_dy * weight
        for c in range(chunks):
            lanes = slice(c * LANES, (c + 1) * LANES)
            stage_ref[:, slot * 2 * chunks + c, :] = rows_x[:, lanes]
            stage_ref[:, slot * 2 * chunks + chunks + c, :] = rows_dy[:, lanes]
    for e in range(experts):
        block = stage_ref[e].astype(jnp.bfloat16)
        for z in range(nz):
            send_ref[e, z] = block


def project_kernel(guest_ref, own_ref, mine_hbm, stack_ref, partial_ref, mine_ref, mine_sem):
    hid = stack_ref.shape[1]
    width = stack_ref.shape[0] // 3
    half = own_ref.shape[0]
    fetch = pltpu.make_async_copy(mine_hbm, mine_ref, mine_sem)
    fetch.start()
    for place, weights_ref in ((1, stack_ref), (0, mine_ref)):
        if place == 0:
            fetch.wait()
        for h, rows_ref in enumerate((guest_ref, own_ref)):
            rows = slice(h * half, (h + 1) * half)
            x = rows_ref[:, :width]
            total = None
            for k in range(width // hid):
                piece = contract(
                    rows_ref[:, width + k * hid : width + (k + 1) * hid],
                    weights_ref[2 * width + k * hid : 2 * width + (k + 1) * hid, :],
                    1,
                    1,
                )
                total = piece if total is None else total + piece
            parts = (
                contract(x, weights_ref[:width, :], 1, 0),
                contract(x, weights_ref[width : 2 * width, :], 1, 0),
                total,
            )
            for k, part in enumerate(parts):
                low = (2 * k + place) * hid
                partial_ref[rows, low : low + hid] = part.astype(jnp.bfloat16)


def pullback_kernel(
    partial_ref, other_ref, mine_hbm, stack_ref,
    pack_ref, hidden_ref, gate_pre_ref, up_pre_ref, score_ref, mine_ref, mine_sem, *, first
):
    hid = stack_ref.shape[1]
    width = stack_ref.shape[0] // 3
    fetch = pltpu.make_async_copy(mine_hbm.at[pl.ds(0, 2 * width), :], mine_ref, mine_sem)
    fetch.start()
    both = 2 * hid
    half = hidden_ref.shape[0]
    step = 16

    def one(i, carry):
        rows = pl.ds(pl.multiple_of(i * step, step), step)
        source = pl.ds(pl.multiple_of(first + i * step, step), step)
        total = partial_ref[source, :].astype(jnp.float32) + other_ref[source, :].astype(jnp.float32)
        gate_pre, up_pre, d_hidden = total[:, :both], total[:, both : 2 * both], total[:, 2 * both :]
        sigmoid_gate = jax.nn.sigmoid(gate_pre)
        silu_gate = gate_pre * sigmoid_gate
        hidden = (silu_gate * up_pre).astype(jnp.bfloat16)
        score = jnp.sum(d_hidden * hidden.astype(jnp.float32), axis=1, keepdims=True)
        hidden_ref[rows, :] = hidden
        gate_pre_ref[rows, :] = (
            d_hidden * up_pre * sigmoid_gate * (1.0 + gate_pre * (1.0 - sigmoid_gate))
        ).astype(jnp.bfloat16)
        up_pre_ref[rows, :] = (d_hidden * silu_gate).astype(jnp.bfloat16)
        score_ref[rows, :] = jnp.broadcast_to(score, (step, LANES))
        return carry

    lax.fori_loop(0, half // step, one, 0)
    fetch.wait()
    pack_ref[:half, :] = (
        contract(gate_pre_ref[:, :hid], mine_ref[:width, :], 1, 1)
        + contract(gate_pre_ref[:, hid:], stack_ref[:width, :], 1, 1)
        + contract(up_pre_ref[:, :hid], mine_ref[width:, :], 1, 1)
        + contract(up_pre_ref[:, hid:], stack_ref[width : 2 * width, :], 1, 1)
    ).astype(jnp.bfloat16)
    extra = pack_ref.shape[0] - half
    pack_ref[half:, :] = jnp.zeros((extra, width), jnp.bfloat16)
    score = score_ref[...]
    a = lax.broadcasted_iota(jnp.int32, (half, LANES), 0)
    b = lax.broadcasted_iota(jnp.int32, (half, LANES), 1)
    for k in range(-(-half // LANES)):
        row = jnp.sum(jnp.where(a == b + k * LANES, score, 0.0), axis=0, keepdims=True)
        pack_ref[half:, k * LANES : (k + 1) * LANES] = jnp.broadcast_to(
            row, (extra, LANES)
        ).astype(jnp.bfloat16)


def products_kernel(*refs, first):
    out_ref = refs[-1]
    groups = (refs[:4], refs[4:8])
    hid = out_ref.shape[1]
    width = refs[0].shape[1] // 2
    part = slice(first, first + hid)

    def product(left, right):
        return sum(contract(left(group), right(group), 0, 0) for group in groups).astype(out_ref.dtype)

    for k in range(width // hid):
        low, high = k * hid, (k + 1) * hid
        out_ref[low:high, :] = product(lambda g: g[0][:, low:high], lambda g: g[2][:, part])
        out_ref[width + low : width + high, :] = product(
            lambda g: g[0][:, low:high], lambda g: g[3][:, part]
        )
        out_ref[2 * width + low : 2 * width + high, :] = product(
            lambda g: g[1][:, part], lambda g: g[0][:, width + low : width + high]
        )


def settle_kernel(
    mine_ref, theirs_hbm, gate_hbm, up_hbm, down_hbm, theirs_ref, wide_ref, tall_ref, in_sem, out_sem
):
    width, hid = gate_hbm.shape[1:]
    loads = []
    for k in range(3):
        rows = pl.ds(k * width, width)
        loads.append(
            pltpu.make_async_copy(theirs_hbm.at[rows, :], theirs_ref.at[rows, :], in_sem.at[k])
        )
        loads[-1].start()

    def total(start, size):
        rows = slice(start, start + size)
        return (mine_ref[rows, :] + theirs_ref[rows, :].astype(jnp.float32)).astype(jnp.bfloat16)

    stores = []
    for k, out in enumerate((gate_hbm, up_hbm)):
        loads[k].wait()
        wide_ref[k] = total(k * width, width)
        stores.append(pltpu.make_async_copy(wide_ref.at[k], out.at[0], out_sem.at[k]))
        stores[-1].start()
    loads[2].wait()
    for k in range(width // hid):
        tall_ref[:, k * hid : (k + 1) * hid] = total(2 * width + k * hid, hid)
    stores.append(pltpu.make_async_copy(tall_ref, down_hbm.at[0], out_sem.at[2]))
    stores[-1].start()
    for store in stores:
        store.wait()


def per_device(tokens, out_grad, expert_ids, gate_probs, w_gate, w_up, w_down):
    experts = lax.axis_size("expert")
    nx = lax.axis_size("x")
    nz = lax.axis_size("z")
    tok_rows, width = tokens.shape
    chunks = width // LANES
    slots = experts * CAP

    probs = gate_probs.astype(jnp.bfloat16).astype(jnp.float32)
    rows_out = CAP * 2 * chunks
    send, position = pl.pallas_call(
        dispatch_kernel,
        out_shape=(
            jax.ShapeDtypeStruct((experts, nz, rows_out, LANES), jnp.bfloat16),
            jax.ShapeDtypeStruct((2, tok_rows), jnp.int32),
        ),
        in_specs=[pl.BlockSpec(memory_space=pltpu.VMEM)] * 4,
        out_specs=(
            pl.BlockSpec(memory_space=pltpu.VMEM),
            pl.BlockSpec(memory_space=pltpu.VMEM),
        ),
        scratch_shapes=[pltpu.VMEM((experts, rows_out, LANES), jnp.float32)],
    )(expert_ids.T, gate_probs.T, tokens, out_grad)
    send = send.reshape(experts * nz, rows_out, LANES)
    slot_names = jnp.arange(slots, dtype=jnp.int32)
    place0 = slot_names[:, None] == position[0][None, :]
    place1 = slot_names[:, None] == position[1][None, :]
    placing = (place0 | place1).astype(jnp.bfloat16)
    part_rows = experts * nz * CAP
    gate_w = w_gate[0]
    up_w = w_up[0]
    down_w = w_down[0]
    hid = gate_w.shape[1]

    def meet(block, mask):
        return lax.ppermute(block, "x", [(i, i ^ mask) for i in range(nx)])

    def swap(block):
        return lax.ppermute(block, "dp", [(0, 1), (1, 0)])

    def stacked(gate, up, down):
        return jnp.concatenate([gate, up] + jnp.split(down, width // hid, axis=1), axis=0)

    own_weights = stacked(gate_w, up_w, down_w)
    weights = meet(own_weights, 1)
    own = exchange(send, ("expert", "z")).reshape(part_rows, 2 * width)
    guest = meet(own, 3)
    own, guest = lax.optimization_barrier((own, guest))

    vmem = pl.BlockSpec(memory_space=pltpu.VMEM)
    params = pltpu.CompilerParams(vmem_limit_bytes=16 << 20)

    hbm = pl.BlockSpec(memory_space=pl.ANY)

    def call(kernel, outs, args, scratch=(), flops=0, far=(), far_out=False):
        return pl.pallas_call(
            kernel,
            out_shape=tuple(jax.ShapeDtypeStruct(s, d) for s, d in outs),
            in_specs=[hbm if k in far else vmem for k in range(len(args))],
            out_specs=tuple(hbm if far_out else vmem for _ in outs),
            scratch_shapes=list(scratch),
            compiler_params=params,
            cost_estimate=pl.CostEstimate(flops=flops, bytes_accessed=6 << 20, transcendentals=0),
        )(*args)

    bf16 = jnp.bfloat16
    all_rows, both = 2 * part_rows, 2 * hid
    dot_flops = 2 * all_rows * width * both
    (partial,) = call(
        project_kernel,
        [((all_rows, 3 * both), bf16)],
        (guest, own, own_weights, weights),
        [pltpu.VMEM((3 * width, hid), bf16), pltpu.SemaphoreType.DMA],
        flops=3 * dot_flops,
        far=(2,),
    )
    pack_rows = part_rows + 16
    other = swap(partial)

    def pulled(first):
        return call(
            functools.partial(pullback_kernel, first=first),
            [((pack_rows, width), bf16)] + [((part_rows, both), bf16)] * 3,
            (partial, other, own_weights, weights),
            [
                pltpu.VMEM((part_rows, LANES), jnp.float32),
                pltpu.VMEM((2 * width, hid), bf16),
                pltpu.SemaphoreType.DMA,
            ],
            flops=dot_flops,
            far=(2,),
        )

    pack_guest, *terms_guest = pulled(0)
    back = meet(pack_guest, 3)
    pack_own, *terms_own = pulled(part_rows)
    terms = (guest, *terms_guest, own, *terms_own)
    (theirs,) = call(
        functools.partial(products_kernel, first=hid),
        [((3 * width, hid), bf16)],
        terms,
        flops=3 * dot_flops // 2,
    )
    theirs = meet(theirs, 1)
    back = (pack_own.astype(jnp.float32) + back.astype(jnp.float32)).astype(bf16)
    (mine,) = call(
        functools.partial(products_kernel, first=0),
        [((3 * width, hid), jnp.float32)],
        terms,
        flops=3 * dot_flops // 2,
    )
    grad_gate, grad_up, grad_down = call(
        settle_kernel,
        [((1, width, hid), bf16), ((1, width, hid), bf16), ((1, hid, width), bf16)],
        (mine, theirs),
        [
            pltpu.VMEM((3 * width, hid), bf16),
            pltpu.VMEM((2, width, hid), bf16),
            pltpu.VMEM((hid, width), bf16),
            pltpu.SemaphoreType.DMA((3,)),
            pltpu.SemaphoreType.DMA((3,)),
        ],
        far=(1,),
        far_out=True,
    )

    data = back[:part_rows].reshape(experts * nz, CAP * chunks, LANES)
    marks = jnp.pad(
        back[part_rows, :part_rows].reshape(experts * nz, 1, CAP),
        ((0, 0), (0, 1), (0, LANES - CAP)),
    )
    home = jnp.concatenate([data, marks], axis=1)
    home = exchange(
        home.reshape(experts * nz, CAP * chunks // 2 + 1, 2, LANES), ("expert", "z")
    )
    home = jnp.sum(
        home.reshape(experts, nz, CAP * chunks + 2, LANES).astype(jnp.float32), axis=1
    )
    pair_rows = home[:, : CAP * chunks].astype(jnp.bfloat16).reshape(slots, width)
    pair_score = home[:, CAP * chunks, :CAP].reshape(slots, 1)
    grad_tokens = contract(placing, pair_rows, 0, 0).astype(jnp.bfloat16)
    score0 = jnp.sum(jnp.where(place0, pair_score, 0.0), axis=0)
    score1 = jnp.sum(jnp.where(place1, pair_score, 0.0), axis=0)
    grad_probs = (jnp.stack([score0, score1], axis=1) / probs).astype(jnp.bfloat16)
    return (grad_tokens, grad_gate, grad_up, grad_down, grad_probs)


def solution(mesh):
    names = dict(zip(mesh.axis_names, mesh.devices.shape))
    nz = 8
    nx = names["ffn"] // nz
    grid = Mesh(
        mesh.devices.reshape(names["expert"], nx, nz, names["dp"]), ("expert", "x", "z", "dp")
    )
    toks = P(("expert", "x", "z"), "dp")
    pairs = P(("expert", "x", "z"), None)
    wide = P("expert", "dp", ("x", "z"))
    tall = P("expert", ("x", "z"), "dp")
    return jax.shard_map(
        per_device,
        mesh=grid,
        in_specs=(toks, toks, pairs, pairs, wide, wide, tall),
        out_specs=(toks, wide, wide, tall, pairs),
        check_vma=False,
    )
```
